512 devices in a mesh: rows: 128 (over x, z, y_hi, core), repl: 4 (over y_lo).
Axes of the slice: x: 4, y: 8 (y_hi: 2, y_lo: 4; y = y_hi * 4 + y_lo), z: 8, core: 2. Of those that a mesh axis runs over, the one named last changes fastest.
Arguments:
- features: bfloat16 [128, 16384], P(None, 'rows'), may hold values from -6 to 6
- tile_blocks: int32 [16384], P(('rows', 'repl')), may hold values from -1 to 127, as said below
- tile_counts: int32 [16384, 128, 128], P(('rows', 'repl')), may hold values from 0 to 3, as said below
- train_mask: int32 [16384], P('rows'), may hold values 0 or 1
- cotangent: bfloat16 [47, 16384], P(None, 'rows'), may hold values from -6 to 6
- self_one: bfloat16 [128, 256], P(None, 'repl'), may hold values from -0.5 to 0.5
- neighbor_one: bfloat16 [128, 256], P(None, 'repl'), may hold values from -1.5 to 1.5
- bias_one: bfloat16 [256], P('repl'), may hold values from -3 to 3
- self_two: bfloat16 [256, 47], P('repl'), may hold values from -0.375 to 0.375
- neighbor_two: bfloat16 [256, 47], P('repl'), may hold values from -1 to 1
- bias_two: bfloat16 [47], replicated, may hold values from -3 to 3
Outputs:
- scores: float32 [47, 16384], P(None, 'rows')
- selfgrad_one: float32 [128, 256], P(None, 'repl')
- neighgrad_one: float32 [128, 256], P(None, 'repl')
- biasgrad_one: float32 [256], P('repl')
- selfgrad_two: float32 [256, 47], P('repl')
- neighgrad_two: float32 [256, 47], P('repl')
- biasgrad_two: float32 [47], replicated
The draws below stay inside these ranges and needn't reach their ends.
Inputs may be any that keep to these rules, and one draw needn't show every extreme that they name: `tile_blocks`: each device's 32 slots hold the column blocks of its live tiles first and -1 after them; every device has at least one live tile, and some device has all 32 live. `tile_counts`: entries count edges; most are zero.
All inputs are finite; a program needn't handle non-finite values. No bound on the sum of `train_mask` on one device may be relied on, other than what follows from the above.
Results may differ from the reference program's by a relative error of at most 0.0045.
Values may be sent and summed in bfloat16 or wider, within the bound.
No kernel may reach another device: no remote copies, remote signals or barrier semaphores. Data moves between devices by JAX's collectives and lax.ppermute only.
A program may use at most 64 MiB of HBM per device.

```python
import jax
import jax.numpy as jnp
from jax import lax

F_IN = 128
HID = 256
CLASSES = 47
TILE = 128
TILES = 32
ODDS = 160
NODES = 16384
BLOCKS = 128
SLOTS = 16384
N_ROWS = 128
N_REPL = 4


def draw_tile_blocks(key, part):
    key = jax.random.fold_in(key, 11)
    keys = jax.random.split(key, 3)
    devices = SLOTS // TILES
    live_count = jax.random.randint(keys[0], (devices,), 1, TILES + 1)
    fullest = jax.random.randint(keys[1], (), 0, devices)
    live_count = jnp.where(jnp.arange(devices) == fullest, TILES, live_count)
    column_blocks = jax.random.randint(keys[2], (devices, TILES), 0, BLOCKS)
    slot_order = jnp.arange(TILES)[None, :]
    chosen = jnp.where(slot_order < live_count[:, None], column_blocks, -1)
    return chosen.reshape(SLOTS).astype(jnp.int32)


def draw_tile_counts(key, part):
    key = jax.random.fold_in(key, 23)
    keys = jax.random.split(key, 2)
    present = jax.random.randint(keys[0], (SLOTS, TILE, TILE), 0, ODDS)
    values = jax.random.randint(keys[1], (SLOTS, TILE, TILE), 1, 4)
    return jnp.where(present == 0, values, 0).astype(jnp.int32)


def plant(values, stream_key, smallest, high):
    longest = values.shape.index(max(values.shape))
    spots = []
    for shift in (0, 1):
        where = [jax.random.randint(jax.random.fold_in(stream_key, axis), (), 0, length) for axis, length in enumerate(values.shape)]
        where[longest] = (where[longest] + shift) % values.shape[longest]
        spots.append(tuple(where))
    return values.at[spots[0]].set(smallest).at[spots[1]].set(high)


def shard_levels(key, dims, cuts, smallest, largest):
    def one(dim, shards_of):
        draws = jax.random.uniform(jax.random.fold_in(jax.random.fold_in(key, 6), dim), (shards_of,), jnp.float32, smallest / len(cuts), largest / len(cuts))
        return jnp.repeat(jnp.exp(draws), dims[dim] // shards_of).reshape((-1,) + (1,) * (len(dims) - dim - 1))

    level = one(*cuts[0])
    for cut in cuts[1:]:
        level = level * one(*cut)
    return level


def centred(own_key, extent, scale, bound, pieces=(), kind=jnp.bfloat16):
    factor_of = shard_levels(own_key, extent, pieces, -0.22, 0.18) if pieces else 1.0
    result = jax.random.normal(own_key, extent, jnp.float32) * scale * factor_of
    return jnp.minimum(jnp.maximum(result, -bound), bound).astype(kind)


def setup_inputs(seed: int = 0) -> dict:
    arg_keys = jax.random.split(jax.random.key(seed), 12)
    features = centred(arg_keys[0], (F_IN, NODES), 1.0, 6.0, ((1, 128),))
    tile_blocks = draw_tile_blocks(jax.random.fold_in(arg_keys[11], 71), 0)
    tile_counts = draw_tile_counts(jax.random.fold_in(arg_keys[11], 71), 0)
    train_mask = plant((jax.random.randint(arg_keys[3], (NODES,), 0, 2) < 1).astype(jnp.int32), jax.random.fold_in(arg_keys[3], 1), 0, 1)
    cotangent = centred(arg_keys[4], (CLASSES, NODES), 1.0, 6.0, ((1, 128),))
    self_one = centred(arg_keys[5], (F_IN, HID), F_IN ** -0.5, 0.5, ((1, 4),))
    neighbor_one = centred(arg_keys[6], (F_IN, HID), (F_IN // 8) ** -0.5, 1.5, ((1, 4),))
    bias_one = centred(arg_keys[7], (HID,), 0.5, 3.0, ((0, 4),))
    self_two = centred(arg_keys[8], (HID, CLASSES), HID ** -0.5, 0.375, ((0, 4),))
    neighbor_two = centred(arg_keys[9], (HID, CLASSES), (HID // 8) ** -0.5, 1.0, ((0, 4),))
    bias_two = centred(arg_keys[10], (CLASSES,), 0.5, 3.0)
    return {"features": features, "tile_blocks": tile_blocks, "tile_counts": tile_counts, "train_mask": train_mask, "cotangent": cotangent, "self_one": self_one, "neighbor_one": neighbor_one, "bias_one": bias_one, "self_two": self_two, "neighbor_two": neighbor_two, "bias_two": bias_two}


def forward_tiles(source, tile_blocks, tile_counts):
    width = source.shape[0]
    group = TILES * N_REPL

    def advance(running, item):
        position, column_block, counts = item
        partition = (position // group).astype(jnp.int32)
        safe_block = jnp.maximum(column_block, 0).astype(jnp.int32)
        columns = lax.dynamic_slice_in_dim(source, safe_block * TILE, TILE, 1)
        product = lax.dot_general(columns, counts.astype(jnp.bfloat16), (((1,), (1,)), ((), ())), preferred_element_type=jnp.float32)
        product = jnp.where(column_block >= 0, product, jnp.zeros_like(product))
        current = lax.dynamic_slice_in_dim(running, partition * TILE, TILE, 1)
        return lax.dynamic_update_slice_in_dim(running, current + product, partition * TILE, 1), None

    initial = jnp.zeros((width, NODES), jnp.float32)
    positions = jnp.arange(SLOTS, dtype=jnp.int32)
    running, unused = lax.scan(advance, initial, (positions, tile_blocks, tile_counts))
    return running


def backward_tiles(scaled, tile_blocks, tile_counts):
    width = scaled.shape[0]
    group = TILES * N_REPL

    def advance(running, item):
        position, column_block, counts = item
        partition = (position // group).astype(jnp.int32)
        safe_block = jnp.maximum(column_block, 0).astype(jnp.int32)
        columns = lax.dynamic_slice_in_dim(scaled, partition * TILE, TILE, 1)
        product = jnp.dot(columns, counts.astype(jnp.bfloat16), preferred_element_type=jnp.float32)
        product = jnp.where(column_block >= 0, product, jnp.zeros_like(product))
        current = lax.dynamic_slice_in_dim(running, safe_block * TILE, TILE, 1)
        return lax.dynamic_update_slice_in_dim(running, current + product, safe_block * TILE, 1), None

    initial = jnp.zeros((width, NODES), jnp.float32)
    positions = jnp.arange(SLOTS, dtype=jnp.int32)
    running, unused = lax.scan(advance, initial, (positions, tile_blocks, tile_counts))
    return running


def reference(features, tile_blocks, tile_counts, train_mask, cotangent, self_one, neighbor_one, bias_one, self_two, neighbor_two, bias_two):
    contract = (((0,), (0,)), ((), ()))
    rowwise = (((1,), (1,)), ((), ()))
    valid = (tile_blocks >= 0).astype(jnp.float32)
    row_counts = jnp.sum(tile_counts, axis=2).astype(jnp.float32) * valid[:, None]
    degree = jnp.sum(row_counts.reshape(N_ROWS, TILES * N_REPL, TILE), axis=1).reshape(NODES)
    inverse = 1.0 / (degree + 1.0)
    mean_one = (forward_tiles(features, tile_blocks, tile_counts) * inverse[None, :]).astype(jnp.bfloat16)
    hidden_pre = lax.dot_general(self_one, features, contract, preferred_element_type=jnp.float32)
    hidden_pre = hidden_pre + lax.dot_general(neighbor_one, mean_one, contract, preferred_element_type=jnp.float32)
    hidden_pre = hidden_pre + bias_one.astype(jnp.float32)[:, None]
    hidden = jax.nn.silu(hidden_pre).astype(jnp.bfloat16)
    projected = lax.dot_general(neighbor_two, hidden, contract, preferred_element_type=jnp.float32).astype(jnp.bfloat16)
    skipped = lax.dot_general(self_two, hidden, contract, preferred_element_type=jnp.float32)
    scores = skipped + forward_tiles(projected, tile_blocks, tile_counts) * inverse[None, :] + bias_two.astype(jnp.float32)[:, None]
    upstream = cotangent * train_mask.astype(jnp.bfloat16)[None, :]
    scaled = (upstream.astype(jnp.float32) * inverse[None, :]).astype(jnp.bfloat16)
    pulled = backward_tiles(scaled, tile_blocks, tile_counts).astype(jnp.bfloat16)
    hidden_grad = jnp.dot(self_two, upstream, preferred_element_type=jnp.float32) + jnp.dot(neighbor_two, pulled, preferred_element_type=jnp.float32)
    sigmoid = jax.nn.sigmoid(hidden_pre)
    pre_grad = (hidden_grad * sigmoid * (1.0 + hidden_pre * (1.0 - sigmoid))).astype(jnp.bfloat16)
    selfgrad_one = lax.dot_general(features, pre_grad, rowwise, preferred_element_type=jnp.float32)
    neighgrad_one = lax.dot_general(mean_one, pre_grad, rowwise, preferred_element_type=jnp.float32)
    biasgrad_one = jnp.sum(pre_grad.astype(jnp.float32), axis=1)
    selfgrad_two = lax.dot_general(hidden, upstream, rowwise, preferred_element_type=jnp.float32)
    neighgrad_two = lax.dot_general(hidden, pulled, rowwise, preferred_element_type=jnp.float32)
    biasgrad_two = jnp.sum(upstream.astype(jnp.float32), axis=1)
    return (scores, selfgrad_one, neighgrad_one, biasgrad_one, selfgrad_two, neighgrad_two, biasgrad_two)
```

```python
import functools

import jax
import jax.numpy as jnp
from jax import lax
from jax.experimental import pallas as pl
from jax.experimental.pallas import tpu as pltpu
from jax.sharding import Mesh, PartitionSpec as P

BF = jnp.bfloat16
F32 = jnp.float32
CLASSES = 47
WIDE = 48
EDGE = 128
ROWS = ("x", "z", "yh", "core")
PLANE = ("x", "z")
COLUMN = ("yh", "yl")
GRADS = 256
VMEM = pl.BlockSpec(memory_space=pltpu.VMEM)
SMEM = pl.BlockSpec(memory_space=pltpu.SMEM)
NT = (((1,), (1,)), ((), ()))
TN = (((0,), (0,)), ((), ()))


def dot(a, b, dims=(((1,), (0,)), ((), ()))):
    return lax.dot_general(a, b, dims, preferred_element_type=F32)


def call(body, outs, in_specs, scratch=()):
    return pl.pallas_call(
        body,
        out_shape=outs,
        in_specs=in_specs,
        out_specs=jax.tree.map(lambda _: VMEM, outs),
        scratch_shapes=list(scratch),
        compiler_params=pltpu.CompilerParams(vmem_limit_bytes=40 * 1024 * 1024),
    )


def halves(value):
    high = value.astype(BF).astype(F32)
    return jnp.concatenate([high, value - high], axis=0).astype(BF)


def prepare_kernel(steps, n_repl, blocks, counts, weights, cat, send, total):
    step = pl.program_id(0)
    per = counts.shape[0]
    for t in range(per):
        live = blocks[step * per + t] >= 0
        tile = jnp.where(live, counts[t], 0).astype(F32).astype(BF)
        cat[:, t * EDGE : (t + 1) * EDGE] = tile
    part = dot(jnp.ones((8, per * EDGE), BF), cat[...], NT)

    @pl.when(step == 0)
    def _():
        total[...] = part

    @pl.when(step > 0)
    def _():
        total[...] += part

    @pl.when(step == steps - 1)
    def _():
        whole = total[0:1]
        high = jnp.floor(whole * (1.0 / 256.0))
        low = whole - high * 256.0
        row = lax.broadcasted_iota(jnp.int32, (16, EDGE), 0)
        both = jnp.where(row == 0, high, jnp.where(row == 1, low, 0.0)).astype(BF)
        for r in range(n_repl):
            send[r, 0:192] = weights[...]
            send[r, 192:208] = both


def spread_kernel(blocks, core, cat, got, cot, mask, mine, other, up_out, inv_out):
    degree = jnp.zeros((1, EDGE), F32)
    for r in range(got.shape[0]):
        both = got[r, 192:208].astype(F32)
        degree = degree + both[0:1] * 256.0 + both[1:2]
    inverse = 1.0 / (degree + 1.0)
    inv_out[...] = jnp.broadcast_to(inverse, inv_out.shape)
    upstream = cot[...].astype(F32) * mask[...].astype(F32)
    up_out[...] = upstream.astype(BF)
    scaled = (upstream * inverse).astype(BF)
    mine[...] = jnp.zeros_like(mine)
    other[...] = jnp.zeros_like(other)
    me = core[0]
    for t in range(cat.shape[1] // EDGE):
        block = jnp.maximum(blocks[t], 0)
        product = dot(scaled, cat[:, t * EDGE : (t + 1) * EDGE])
        own = (block & 1) == me
        at = block >> 1
        mine[at] += jnp.where(own, product, 0.0)
        other[at] += jnp.where(own, 0.0, product)


def plane_sum_kernel(got, send):
    n_repl = send.shape[0] * WIDE // got.shape[1]
    total = got[0].astype(F32)
    for j in range(1, got.shape[0]):
        total = total + got[j].astype(F32)
    for h in range(got.shape[1] // WIDE):
        piece = total[h * WIDE : (h + 1) * WIDE].astype(BF)
        for r in range(n_repl):
            send[h * n_repl + r] = piece


def gather_one_kernel(blocks, core, own, far, cat, send, picked):
    me = core[0]
    n_repl, part = send.shape[0], own.shape[2]
    for t in range(cat.shape[1] // EDGE):
        block = jnp.maximum(blocks[t], 0)
        half = (block >> 1) & 1
        at = block >> 2
        near = (block & 1) == me
        for q in range(n_repl):
            a = own[half * n_repl + q, at]
            b = far[half * n_repl + q, at]
            picked[q * part : (q + 1) * part, t * EDGE : (t + 1) * EDGE] = jnp.where(near, a, b)
    total = dot(picked[...], cat[...], NT)
    for r in range(n_repl):
        send[r] = total


def layer_kernel(repl, parts, got, back, up, inv, features, send, skipped, packed):
    plane = send.shape[0]
    chunk = GRADS // plane
    total = parts[0]
    for r in range(1, parts.shape[0]):
        total = total + parts[r]
    mean = (total * inv[0:1]).astype(BF)
    feat = features[...]

    def before(r):
        bias = got[r, 128:192][:, 2 * WIDE - 1 : 2 * WIDE].astype(F32)
        return (dot(got[r, 0:64], feat) + dot(got[r, 64:128], mean)) + bias

    projections = jnp.zeros((EDGE, EDGE), F32)
    for r in range(parts.shape[0]):
        pre = before(r)
        hidden = (pre * jax.nn.sigmoid(pre)).astype(BF)
        projections = projections + dot(got[r, 128:192], hidden, TN)
    skipped[...] = projections[WIDE : 2 * WIDE]
    projected = projections[0:WIDE].astype(BF)

    pulled = back[0].astype(F32)
    for r in range(1, back.shape[0]):
        pulled = pulled + back[r].astype(F32)
    upstream = up[...]
    right = jnp.concatenate(
        [pulled, upstream.astype(F32), jnp.zeros((EDGE - 2 * WIDE, EDGE), F32)], axis=0
    ).astype(BF)
    mine = repl[0]
    pre = before(mine)
    sigmoid = jax.nn.sigmoid(pre)
    hidden = (pre * sigmoid).astype(BF)
    hidden_grad = dot(got[mine, 128:192], right)
    pre_grad = (hidden_grad * sigmoid * (1.0 + pre * (1.0 - sigmoid))).astype(BF)
    lane = lax.broadcasted_iota(jnp.int32, (EDGE, EDGE), 1)
    twice = jnp.concatenate([pre_grad, pre_grad], axis=0)
    packed[0:128] = jnp.where(lane < 64, dot(feat, twice, NT), dot(mean, twice, NT))
    bias_one = jnp.sum(pre_grad.astype(F32), axis=1, keepdims=True)
    bias_two = jnp.sum(upstream.astype(F32), axis=1, keepdims=True)
    bias_two = jnp.concatenate([bias_two, jnp.zeros((64 - WIDE, 1), F32)], axis=0)
    second = dot(hidden, right, NT)
    lane = lane[0:64]
    second = jnp.where(lane == 96, bias_one, jnp.where(lane == 97, bias_two, second))
    packed[128:192] = second
    packed[192:256] = jnp.zeros((64, EDGE), F32)
    for j in range(plane):
        send[j, 0:WIDE] = projected
        send[j, WIDE : WIDE + 2 * chunk] = halves(packed[j * chunk : (j + 1) * chunk])


def relay_kernel(repl, got, send):
    share = (send.shape[1] - (got.shape[1] - WIDE)) // WIDE
    chunk = (got.shape[1] - WIDE) // 2
    total = got[0, WIDE:].astype(F32)
    for j in range(1, got.shape[0]):
        total = total + got[j, WIDE:].astype(F32)
    both = halves(total[0:chunk] + total[chunk:])
    first = repl[0] * share
    for j in range(share):
        piece = got[first + j, 0:WIDE]
        for d in range(send.shape[0]):
            send[d, j * WIDE : (j + 1) * WIDE] = piece
    for d in range(send.shape[0]):
        send[d, share * WIDE :] = both


def gather_two_kernel(blocks, core, repl, own, far, cat, send, grads, picked):
    me = core[0]
    n_repl = send.shape[0]
    chunk = grads.shape[1]
    share = (own.shape[1] - 2 * chunk) // WIDE
    for t in range(cat.shape[1] // EDGE):
        block = jnp.maximum(blocks[t], 0)
        half = (block >> 1) & 1
        plane = block >> 2
        owner = plane // share
        at = pl.multiple_of((plane - owner * share) * WIDE, 16)
        near = (block & 1) == me
        a = own[half * n_repl + owner, pl.ds(at, WIDE)]
        b = far[half * n_repl + owner, pl.ds(at, WIDE)]
        picked[:, t * EDGE : (t + 1) * EDGE] = jnp.where(near, a, b)
    total = dot(picked[...], cat[...], NT)
    for r in range(n_repl):
        send[r] = total
    sums = []
    for ref in (own, far):
        both = jnp.zeros((2 * chunk, EDGE), F32)
        for h in range(own.shape[0] // n_repl):
            both = both + ref[h * n_repl + repl[0], share * WIDE :].astype(F32)
        sums.append(both[0:chunk] + both[chunk:])
    whole = sums[0] + sums[1]
    for j in range(grads.shape[0]):
        grads[j] = whole


def per_device(
    sizes,
    features,
    tile_blocks,
    tile_counts,
    train_mask,
    cotangent,
    self_one,
    neighbor_one,
    bias_one,
    self_two,
    neighbor_two,
    bias_two,
):
    n_repl = sizes["yl"]
    plane = sizes["x"] * sizes["z"]
    halves_n = sizes["yh"]
    column = halves_n * n_repl
    tiles = tile_counts.shape[0]
    chunk = GRADS // plane
    share = plane // n_repl
    core = lax.axis_index("core").astype(jnp.int32).reshape(1)
    repl = lax.axis_index("yl").astype(jnp.int32).reshape(1)
    swap = [(0, 1), (1, 0)]

    part = features.shape[0] // n_repl
    quarter = lax.dynamic_slice_in_dim(features, repl[0] * part, part, 0)
    quarters = lax.all_to_all(
        jnp.broadcast_to(quarter[None], (plane, part, EDGE)), PLANE, 0, 0, tiled=True
    )
    tile_counts, quarters = lax.optimization_barrier((tile_counts, quarters))
    near = lax.all_gather(quarters.reshape(plane * part, EDGE), COLUMN, axis=0, tiled=True)

    second = jnp.concatenate(
        [
            neighbor_two,
            jnp.zeros((64, WIDE - CLASSES), BF),
            self_two,
            bias_one[:, None],
            jnp.zeros((64, EDGE - 2 * WIDE), BF),
        ],
        axis=1,
    )
    weights = jnp.concatenate([self_one.T, neighbor_one.T, second], axis=0)
    steps = 4
    per = tiles // steps
    cat, send = pl.pallas_call(
        functools.partial(prepare_kernel, steps, n_repl),
        grid=(steps,),
        out_shape=(
            jax.ShapeDtypeStruct((EDGE, tiles * EDGE), BF),
            jax.ShapeDtypeStruct((n_repl, 208, EDGE), BF),
        ),
        in_specs=[
            SMEM,
            pl.BlockSpec((per, EDGE, EDGE), lambda i: (i, 0, 0)),
            pl.BlockSpec((192, EDGE), lambda i: (0, 0)),
        ],
        out_specs=(
            pl.BlockSpec((EDGE, per * EDGE), lambda i: (0, i)),
            pl.BlockSpec((n_repl, 208, EDGE), lambda i: (0, 0, 0)),
        ),
        scratch_shapes=[pltpu.VMEM((8, EDGE), F32)],
    )(tile_blocks, tile_counts, weights)
    got = lax.all_to_all(send, "yl", 0, 0, tiled=True)

    cot = jnp.pad(cotangent, ((0, WIDE - CLASSES), (0, 0)))
    mine, other, up, inv = call(
        spread_kernel,
        (
            jax.ShapeDtypeStruct((plane * halves_n, WIDE, EDGE), F32),
            jax.ShapeDtypeStruct((plane * halves_n, WIDE, EDGE), F32),
            jax.ShapeDtypeStruct((WIDE, EDGE), BF),
            jax.ShapeDtypeStruct((8, EDGE), F32),
        ),
        [SMEM, SMEM] + [VMEM] * 4,
    )(tile_blocks, core, cat, got, cot, train_mask[None, :])
    back = (mine + lax.ppermute(other, "core", swap)).astype(BF)
    back = lax.all_to_all(back.reshape(plane, halves_n * WIDE, EDGE), PLANE, 0, 0, tiled=True)
    back = call(plane_sum_kernel, jax.ShapeDtypeStruct((column, WIDE, EDGE), BF), [VMEM])(back)
    back = lax.all_to_all(back, COLUMN, 0, 0, tiled=True)

    far = lax.ppermute(near, "core", swap)
    shape = (column, plane, part, EDGE)
    parts = call(
        gather_one_kernel,
        jax.ShapeDtypeStruct((n_repl, EDGE, EDGE), F32),
        [SMEM, SMEM] + [VMEM] * 3,
        [pltpu.VMEM((EDGE, tiles * EDGE), BF)],
    )(tile_blocks, core, near.reshape(shape), far.reshape(shape), cat)
    parts = lax.all_to_all(parts, "yl", 0, 0, tiled=True)

    send, skipped = call(
        layer_kernel,
        (
            jax.ShapeDtypeStruct((plane, WIDE + 2 * chunk, EDGE), BF),
            jax.ShapeDtypeStruct((WIDE, EDGE), F32),
        ),
        [SMEM] + [VMEM] * 6,
        [pltpu.VMEM((GRADS, EDGE), F32)],
    )(repl, parts, got, back, up, inv, features)

    relay = lax.all_to_all(send, PLANE, 0, 0, tiled=True)
    relay = call(
        relay_kernel,
        jax.ShapeDtypeStruct((column, share * WIDE + 2 * chunk, EDGE), BF),
        [SMEM, VMEM],
    )(repl, relay)
    near_two = lax.all_to_all(relay, COLUMN, 0, 0, tiled=True)
    far_two = lax.ppermute(near_two, "core", swap)
    second_parts, grads = call(
        gather_two_kernel,
        (
            jax.ShapeDtypeStruct((n_repl, WIDE, EDGE), F32),
            jax.ShapeDtypeStruct((plane, chunk, EDGE), F32),
        ),
        [SMEM] * 3 + [VMEM] * 3,
        [pltpu.VMEM((WIDE, tiles * EDGE), BF)],
    )(tile_blocks, core, repl, near_two, far_two, cat)
    second_parts = lax.all_to_all(second_parts, "yl", 0, 0, tiled=True)
    grads = lax.all_to_all(grads, PLANE, 0, 0, tiled=True).reshape(GRADS, EDGE)

    second_sum = jnp.sum(second_parts, axis=0)
    scores = skipped + second_sum * inv[0:1]
    scores = scores[:CLASSES] + bias_two.astype(F32)[:, None]
    return (
        scores,
        grads[0:128, 0:64],
        grads[0:128, 64:128],
        grads[128:192, 96],
        grads[128:192, WIDE : WIDE + CLASSES],
        grads[128:192, 0:CLASSES],
        grads[128 : 128 + CLASSES, 97],
    )


def solution(mesh):
    sizes = {"x": 4, "z": 8, "yh": 2, "core": 2, "yl": 4}
    fine = Mesh(mesh.devices.reshape(tuple(sizes.values())), tuple(sizes))
    return sharded(fine, sizes)


def sharded(fine, sizes):
    both = ROWS + ("yl",)
    return jax.shard_map(
        functools.partial(per_device, sizes),
        mesh=fine,
        in_specs=(
            P(None, ROWS),
            P(both),
            P(both, None, None),
            P(ROWS),
            P(None, ROWS),
            P(None, "yl"),
            P(None, "yl"),
            P("yl"),
            P("yl", None),
            P("yl", None),
            P(),
        ),
        out_specs=(
            P(None, ROWS),
            P(None, "yl"),
            P(None, "yl"),
            P("yl"),
            P("yl", None),
            P("yl", None),
            P(),
        ),
        check_vma=False,
    )
```

```python
import functools

import jax
import jax.numpy as jnp
from jax import lax
from jax.experimental import pallas as pl
from jax.experimental.pallas import tpu as pltpu
from jax.sharding import Mesh, PartitionSpec as P

BF = jnp.bfloat16
F32 = jnp.float32
CLASSES = 47
WIDE = 48
EDGE = 128
ROWS = ("x", "z", "yh", "core")
PLANE = ("x", "z")
COLUMN = ("yh", "yl")
GRADS = 256
VMEM = pl.BlockSpec(memory_space=pltpu.VMEM)
SMEM = pl.BlockSpec(memory_space=pltpu.SMEM)
NT = (((1,), (1,)), ((), ()))
TN = (((0,), (0,)), ((), ()))


def dot(a, b, dims=(((1,), (0,)), ((), ()))):
    return lax.dot_general(a, b, dims, preferred_element_type=F32)


def call(body, outs, in_specs, scratch=()):
    return pl.pallas_call(
        body,
        out_shape=outs,
        in_specs=in_specs,
        out_specs=jax.tree.map(lambda _: VMEM, outs),
        scratch_shapes=list(scratch),
        compiler_params=pltpu.CompilerParams(vmem_limit_bytes=40 * 1024 * 1024),
    )


def halves(value):
    high = value.astype(BF).astype(F32)
    return jnp.concatenate([high, value - high], axis=0).astype(BF)


def prepare_kernel(
    steps, n_repl, blocks, counts, self_one, neighbor_one, neighbor_two, self_two, bias, cat, send, total, second
):
    step = pl.program_id(0)
    per = counts.shape[0]

    @pl.when(step == 0)
    def _():
        total[...] = jnp.zeros_like(total)

    running = total[...]
    for t in range(per):
        live = blocks[step * per + t] >= 0
        tile = jnp.where(live, counts[t], 0).astype(F32)
        cat[:, t * EDGE : (t + 1) * EDGE] = tile.astype(BF)
        running = running + tile
    total[...] = running

    @pl.when(step == steps - 1)
    def _():
        whole = dot(jnp.ones((8, EDGE), BF), running.astype(BF), NT)[0:1]
        high = jnp.floor(whole * (1.0 / 256.0))
        low = whole - high * 256.0
        row = lax.broadcasted_iota(jnp.int32, (16, EDGE), 0)
        both = jnp.where(row == 0, high, jnp.where(row == 1, low, 0.0)).astype(BF)
        second[...] = jnp.zeros_like(second)
        second[0:CLASSES, 0:64] = neighbor_two[...].astype(F32)
        second[CLASSES:WIDE, 0:64] = bias[...].astype(F32)
        second[0:CLASSES, 64:128] = self_two[...].astype(F32)
        layer_two = second[...].astype(BF)
        for r in range(n_repl):
            send[r, 0:64] = self_one[...]
            send[r, 64:128] = neighbor_one[...]
            send[r, 128:176] = layer_two
            send[r, 176:192] = both


def spread_kernel(blocks, core, cat, got, cot, mask, mine, other, up_out, inv_out, far):
    degree = jnp.zeros((1, EDGE), F32)
    for r in range(got.shape[0]):
        both = got[r, 176:192].astype(F32)
        degree = degree + both[0:1] * 256.0 + both[1:2]
    inverse = 1.0 / (degree + 1.0)
    inv_out[...] = jnp.broadcast_to(inverse, inv_out.shape)
    upstream = cot[...].astype(F32) * mask[...].astype(F32)
    up_out[...] = upstream.astype(BF)
    scaled = (upstream * inverse).astype(BF)
    mine[...] = jnp.zeros_like(mine)
    far[...] = jnp.zeros_like(far)
    me = core[0]
    for t in range(cat.shape[1] // EDGE):
        block = jnp.maximum(blocks[t], 0)
        product = dot(scaled, cat[:, t * EDGE : (t + 1) * EDGE])
        own = (block & 1) == me
        at = block >> 1
        mine[at] += jnp.where(own, product, 0.0)
        far[at] += jnp.where(own, 0.0, product)
    other[...] = far[...].astype(BF)


def pair_sum_kernel(mine, other, total):
    total[...] = (mine[...] + other[...].astype(F32)).astype(BF)


def plane_sum_kernel(got, send):
    n_repl = send.shape[0] * WIDE // got.shape[1]
    total = got[0].astype(F32)
    for j in range(1, got.shape[0]):
        total = total + got[j].astype(F32)
    for h in range(got.shape[1] // WIDE):
        piece = total[h * WIDE : (h + 1) * WIDE].astype(BF)
        for r in range(n_repl):
            send[h * n_repl + r] = piece


def gather_one_kernel(blocks, core, own, far, cat, send, picked):
    me = core[0]
    n_repl, part = send.shape[0], own.shape[2]
    for t in range(cat.shape[1] // EDGE):
        block = jnp.maximum(blocks[t], 0)
        half = (block >> 1) & 1
        at = block >> 2
        near = (block & 1) == me
        for q in range(n_repl):
            a = own[half * n_repl + q, at]
            b = far[half * n_repl + q, at]
            picked[q * part : (q + 1) * part, t * EDGE : (t + 1) * EDGE] = jnp.where(near, a, b)
    total = dot(picked[...], cat[...], NT)
    for r in range(n_repl):
        send[r] = total


def layer_kernel(repl, parts, got, back, up, inv, features, bias_two, send, base, packed, pad):
    plane = send.shape[0]
    chunk = GRADS // plane
    total = parts[0]
    for r in range(1, parts.shape[0]):
        total = total + parts[r]
    mean = (total * inv[0:1]).astype(BF)
    feat = features[...]
    last = lax.broadcasted_iota(jnp.int32, (WIDE, EDGE), 0) == CLASSES
    unit = jnp.where(last, 1.0, 0.0).astype(BF)
    none = jnp.zeros((64, EDGE), BF)

    def before(r):
        bias = dot(got[r, 128:176], unit, TN)[0:64]
        return (dot(got[r, 0:64], feat) + dot(got[r, 64:128], mean)) + bias

    projected = jnp.zeros((WIDE, EDGE), F32)
    skipped = jnp.zeros((WIDE, EDGE), F32)
    for r in range(parts.shape[0]):
        pre = before(r)
        hidden = (pre * jax.nn.sigmoid(pre)).astype(BF)
        projected = projected + dot(got[r, 128:176], jnp.concatenate([hidden, none], axis=0))
        skipped = skipped + dot(got[r, 128:176], jnp.concatenate([none, hidden], axis=0))
    projected = projected.astype(BF)
    pad[...] = jnp.zeros_like(pad)
    pad[0:1, 0:CLASSES] = bias_two[...].astype(F32)
    base[...] = skipped + dot(pad[...].astype(BF), jnp.ones((8, EDGE), BF), TN)[0:WIDE]

    pulled = back[0].astype(F32)
    for r in range(1, back.shape[0]):
        pulled = pulled + back[r].astype(F32)
    pulled = pulled.astype(BF)
    upstream = up[...]
    mine = repl[0]
    pre = before(mine)
    sigmoid = jax.nn.sigmoid(pre)
    hidden = (pre * sigmoid).astype(BF)
    second = got[mine, 128:176]
    hidden_grad = dot(second, upstream, TN)[64:128] + dot(second, pulled, TN)[0:64]
    pre_grad = (hidden_grad * sigmoid * (1.0 + pre * (1.0 - sigmoid))).astype(BF)
    packed[0:64] = dot(pre_grad, feat, NT)
    packed[64:128] = dot(pre_grad, mean, NT)
    ones = jnp.ones((8, EDGE), BF)
    twice = jnp.concatenate([hidden, hidden], axis=0)
    left = lax.broadcasted_iota(jnp.int32, (WIDE, EDGE), 1) < 64
    grads_two = jnp.where(left, dot(pulled, twice, NT), dot(upstream, twice, NT))
    bias_one = dot(ones, jnp.concatenate([pre_grad, none], axis=0), NT)[0:1]
    packed[128:176] = jnp.where(last, bias_one, grads_two)
    packed[176:184] = dot(ones, jnp.concatenate([upstream, jnp.zeros((EDGE - WIDE, EDGE), BF)], axis=0), NT)
    packed[184:256] = jnp.zeros((72, EDGE), F32)
    for j in range(plane):
        send[j, 0:WIDE] = projected
        send[j, WIDE : WIDE + 2 * chunk] = halves(packed[j * chunk : (j + 1) * chunk])


def relay_kernel(repl, got, send):
    share = (send.shape[1] - (got.shape[1] - WIDE)) // WIDE
    chunk = (got.shape[1] - WIDE) // 2
    total = got[0, WIDE:].astype(F32)
    for j in range(1, got.shape[0]):
        total = total + got[j, WIDE:].astype(F32)
    both = halves(total[0:chunk] + total[chunk:])
    first = repl[0] * share
    for j in range(share):
        piece = got[first + j, 0:WIDE]
        for d in range(send.shape[0]):
            send[d, j * WIDE : (j + 1) * WIDE] = piece
    for d in range(send.shape[0]):
        send[d, share * WIDE :] = both


def gather_two_kernel(blocks, core, repl, own, far, cat, send, grads, picked):
    me = core[0]
    n_repl = own.shape[0] // 2
    chunk = grads.shape[1]
    share = (own.shape[1] - 2 * chunk) // WIDE
    for t in range(cat.shape[1] // EDGE):
        block = jnp.maximum(blocks[t], 0)
        half = (block >> 1) & 1
        plane = block >> 2
        owner = plane // share
        at = pl.multiple_of((plane - owner * share) * WIDE, 16)
        near = (block & 1) == me
        a = own[half * n_repl + owner, pl.ds(at, WIDE)]
        b = far[half * n_repl + owner, pl.ds(at, WIDE)]
        picked[:, t * EDGE : (t + 1) * EDGE] = jnp.where(near, a, b)
    send[...] = dot(picked[...], cat[...], NT)
    sums = []
    for ref in (own, far):
        both = jnp.zeros((2 * chunk, EDGE), F32)
        for h in range(own.shape[0] // n_repl):
            both = both + ref[h * n_repl + repl[0], share * WIDE :].astype(F32)
        sums.append(both[0:chunk] + both[chunk:])
    whole = sums[0] + sums[1]
    for j in range(grads.shape[0]):
        grads[j] = whole


def scores_kernel(repl, own, first, second, third, base, inv, scores, parts):
    n_repl = parts.shape[0]
    for k, ref in enumerate((own, first, second, third)[:n_repl]):
        at = repl[0] + k
        parts[jnp.where(at >= n_repl, at - n_repl, at)] = ref[...]
    total = parts[0]
    for r in range(1, n_repl):
        total = total + parts[r]
    scores[...] = (base[...] + total * inv[0:1])[0:CLASSES]


def unpack_kernel(grads, self_one, neighbor_one, bias_one, self_two, neighbor_two, bias_two):
    self_one[...] = grads[0:64]
    neighbor_one[...] = grads[64:128]
    neighbor_two[...] = grads[128 : 128 + CLASSES, 0:64]
    self_two[...] = grads[128 : 128 + CLASSES, 64:128]
    bias_one[...] = grads[175:176, 0:64]
    bias_two[...] = grads[176:177, 0:CLASSES]


def per_device(
    sizes,
    features,
    tile_blocks,
    tile_counts,
    train_mask,
    cotangent,
    self_one,
    neighbor_one,
    bias_one,
    self_two,
    neighbor_two,
    bias_two,
):
    n_repl = sizes["yl"]
    plane = sizes["x"] * sizes["z"]
    halves_n = sizes["yh"]
    column = halves_n * n_repl
    tiles = tile_counts.shape[0]
    chunk = GRADS // plane
    share = plane // n_repl
    core = lax.axis_index("core").astype(jnp.int32).reshape(1)
    repl = lax.axis_index("yl").astype(jnp.int32).reshape(1)
    swap = [(0, 1), (1, 0)]

    part = features.shape[0] // n_repl
    quarter = lax.dynamic_slice_in_dim(features, repl[0] * part, part, 0)
    quarters = lax.all_to_all(
        jnp.broadcast_to(quarter[None], (plane, part, EDGE)), PLANE, 0, 0, tiled=True
    )
    tile_counts, quarters = lax.optimization_barrier((tile_counts, quarters))
    near = lax.all_gather(quarters.reshape(plane * part, EDGE), COLUMN, axis=0, tiled=True)

    steps = 4
    per = tiles // steps
    whole = lambda shape: pl.BlockSpec(shape, lambda i: (0,) * len(shape))
    cat, send = pl.pallas_call(
        functools.partial(prepare_kernel, steps, n_repl),
        grid=(steps,),
        out_shape=(
            jax.ShapeDtypeStruct((EDGE, tiles * EDGE), BF),
            jax.ShapeDtypeStruct((n_repl, 192, EDGE), BF),
        ),
        in_specs=[
            SMEM,
            pl.BlockSpec((per, EDGE, EDGE), lambda i: (i, 0, 0)),
            whole((64, EDGE)),
            whole((64, EDGE)),
            whole((CLASSES, 64)),
            whole((CLASSES, 64)),
            whole((1, 64)),
        ],
        out_specs=(
            pl.BlockSpec((EDGE, per * EDGE), lambda i: (0, i)),
            whole((n_repl, 192, EDGE)),
        ),
        scratch_shapes=[pltpu.VMEM((EDGE, EDGE), F32), pltpu.VMEM((WIDE, EDGE), F32)],
    )(
        tile_blocks,
        tile_counts,
        self_one.T,
        neighbor_one.T,
        neighbor_two.T,
        self_two.T,
        bias_one[None, :],
    )
    got = lax.all_to_all(send, "yl", 0, 0, tiled=True)

    cot = jnp.pad(cotangent, ((0, WIDE - CLASSES), (0, 0)))
    mine, other, up, inv = call(
        spread_kernel,
        (
            jax.ShapeDtypeStruct((plane * halves_n, WIDE, EDGE), F32),
            jax.ShapeDtypeStruct((plane * halves_n, WIDE, EDGE), BF),
            jax.ShapeDtypeStruct((WIDE, EDGE), BF),
            jax.ShapeDtypeStruct((8, EDGE), F32),
        ),
        [SMEM, SMEM] + [VMEM] * 4,
        [pltpu.VMEM((plane * halves_n, WIDE, EDGE), F32)],
    )(tile_blocks, core, cat, got, cot, train_mask[None, :])
    back = call(
        pair_sum_kernel,
        jax.ShapeDtypeStruct((plane * halves_n, WIDE, EDGE), BF),
        [VMEM] * 2,
    )(mine, lax.ppermute(other, "core", swap))
    back = lax.all_to_all(back.reshape(plane, halves_n * WIDE, EDGE), PLANE, 0, 0, tiled=True)
    near, back = lax.optimization_barrier((near, back))
    far = lax.ppermute(near, "core", swap)
    back = call(plane_sum_kernel, jax.ShapeDtypeStruct((column, WIDE, EDGE), BF), [VMEM])(back)
    back = lax.all_to_all(back, COLUMN, 0, 0, tiled=True)

    shape = (column, plane, part, EDGE)
    parts = call(
        gather_one_kernel,
        jax.ShapeDtypeStruct((n_repl, EDGE, EDGE), F32),
        [SMEM, SMEM] + [VMEM] * 3,
        [pltpu.VMEM((EDGE, tiles * EDGE), BF)],
    )(tile_blocks, core, near.reshape(shape), far.reshape(shape), cat)
    parts = lax.all_to_all(parts, "yl", 0, 0, tiled=True)

    send, base = call(
        layer_kernel,
        (
            jax.ShapeDtypeStruct((plane, WIDE + 2 * chunk, EDGE), BF),
            jax.ShapeDtypeStruct((WIDE, EDGE), F32),
        ),
        [SMEM] + [VMEM] * 7,
        [pltpu.VMEM((GRADS, EDGE), F32), pltpu.VMEM((8, EDGE), F32)],
    )(repl, parts, got, back, up, inv, features, bias_two[None, :])

    relay = lax.all_to_all(send, PLANE, 0, 0, tiled=True)
    relay = call(
        relay_kernel,
        jax.ShapeDtypeStruct((column, share * WIDE + 2 * chunk, EDGE), BF),
        [SMEM, VMEM],
    )(repl, relay)
    near_two = lax.all_to_all(relay, COLUMN, 0, 0, tiled=True)
    far_two = lax.ppermute(near_two, "core", swap)
    second, grads = call(
        gather_two_kernel,
        (
            jax.ShapeDtypeStruct((WIDE, EDGE), F32),
            jax.ShapeDtypeStruct((plane, chunk, EDGE), F32),
        ),
        [SMEM] * 3 + [VMEM] * 3,
        [pltpu.VMEM((WIDE, tiles * EDGE), BF)],
    )(tile_blocks, core, repl, near_two, far_two, cat)
    others = [
        lax.ppermute(second, "yl", [((i + k) % n_repl, i) for i in range(n_repl)])
        for k in range(1, n_repl)
    ]
    grads = lax.all_to_all(grads, PLANE, 0, 0, tiled=True).reshape(GRADS, EDGE)
    others = others + [second] * (3 - len(others))
    scores = call(
        scores_kernel,
        jax.ShapeDtypeStruct((CLASSES, EDGE), F32),
        [SMEM] + [VMEM] * 6,
        [pltpu.VMEM((n_repl, WIDE, EDGE), F32)],
    )(repl, second, *others, base, inv)
    one = jax.ShapeDtypeStruct((64, EDGE), F32)
    two = jax.ShapeDtypeStruct((CLASSES, 64), F32)
    self_one, neighbor_one, bias_one, self_two, neighbor_two, bias_two = call(
        unpack_kernel,
        (
            one,
            one,
            jax.ShapeDtypeStruct((1, 64), F32),
            two,
            two,
            jax.ShapeDtypeStruct((1, CLASSES), F32),
        ),
        [VMEM],
    )(grads)
    return (
        scores,
        self_one.T,
        neighbor_one.T,
        bias_one[0],
        self_two.T,
        neighbor_two.T,
        bias_two[0],
    )


def solution(mesh):
    sizes = {"x": 4, "z": 8, "yh": 2, "core": 2, "yl": 4}
    fine = Mesh(mesh.devices.reshape(tuple(sizes.values())), tuple(sizes))
    return sharded(fine, sizes)


def sharded(fine, sizes):
    both = ROWS + ("yl",)
    return jax.shard_map(
        functools.partial(per_device, sizes),
        mesh=fine,
        in_specs=(
            P(None, ROWS),
            P(both),
            P(both, None, None),
            P(ROWS),
            P(None, ROWS),
            P(None, "yl"),
            P(None, "yl"),
            P("yl"),
            P("yl", None),
            P("yl", None),
            P(),
        ),
        out_specs=(
            P(None, ROWS),
            P(None, "yl"),
            P(None, "yl"),
            P("yl"),
            P("yl", None),
            P("yl", None),
            P(),
        ),
        check_vma=False,
    )
```

```python
import functools

import jax
import jax.numpy as jnp
from jax import lax
from jax.experimental import pallas as pl
from jax.experimental.pallas import tpu as pltpu
from jax.sharding import Mesh, PartitionSpec as P

BF = jnp.bfloat16
F32 = jnp.float32
CLASSES = 47
WIDE = 48
EDGE = 128
ROWS = ("x", "z", "yh", "core")
PLANE = ("x", "z")
COLUMN = ("yh", "yl")
SHEET = ("z", "yh")
GRADS = 256
VMEM = pl.BlockSpec(memory_space=pltpu.VMEM)
SMEM = pl.BlockSpec(memory_space=pltpu.SMEM)
NT = (((1,), (1,)), ((), ()))
TN = (((0,), (0,)), ((), ()))


def dot(a, b, dims=(((1,), (0,)), ((), ()))):
    return lax.dot_general(a, b, dims, preferred_element_type=F32)


def call(body, outs, in_specs, scratch=(), room=40):
    return pl.pallas_call(
        body,
        out_shape=outs,
        in_specs=in_specs,
        out_specs=jax.tree.map(lambda _: VMEM, outs),
        scratch_shapes=list(scratch),
        compiler_params=pltpu.CompilerParams(vmem_limit_bytes=room * 1024 * 1024),
    )


def halves(value):
    high = value.astype(BF).astype(F32)
    return jnp.concatenate([high, value - high], axis=0).astype(BF)


def lay_kernel(blocks, counts, cat):
    for t in range(counts.shape[0]):
        tile = jnp.where(blocks[t] >= 0, counts[t], 0).astype(F32)
        cat[:, t * EDGE : (t + 1) * EDGE] = tile.astype(BF)


def prepare_kernel(blocks, order, counts, one, two, three, four, five, send, *scratch):
    held, self_one, neighbor_one, neighbor_two, self_two, bias, second, done, ready = scratch
    steps = done.shape[0]
    per = held.shape[0] // steps
    copies = [
        pltpu.make_async_copy(
            counts.at[pl.ds(i * per, per)], held.at[pl.ds(i * per, per)], done.at[i]
        )
        for i in range(steps)
    ]
    pairs = zip((one, two, three, four, five), scratch[1:6])
    weights = [pltpu.make_async_copy(a, b, ready.at[i]) for i, (a, b) in enumerate(pairs)]
    for copy in copies + weights:
        copy.start()
    running = jnp.zeros((EDGE, EDGE), jnp.int32)
    for i, copy in enumerate(copies):
        copy.wait()
        for t in range(i * per, (i + 1) * per):
            running = running + jnp.where(blocks[t] >= 0, held[t], 0)
    for copy in weights:
        copy.wait()
    whole = dot(jnp.ones((8, EDGE), BF), running.astype(F32).astype(BF), NT)[0:1]
    high = jnp.floor(whole * (1.0 / 256.0))
    low = whole - high * 256.0
    row = lax.broadcasted_iota(jnp.int32, (16, EDGE), 0)
    both = jnp.where(row == 0, high, jnp.where(row == 1, low, 0.0)).astype(BF)
    second[...] = jnp.zeros_like(second)
    second[0:CLASSES, 0:64] = neighbor_two[...].astype(F32)
    second[CLASSES:WIDE, 0:64] = bias[...].astype(F32)
    second[0:CLASSES, 64:128] = self_two[...].astype(F32)
    layer_two = second[...].astype(BF)
    for r in range(send.shape[0]):
        send[r, 0:64] = self_one[...]
        send[r, 64:128] = neighbor_one[...]
        send[r, 128:176] = layer_two
        send[r, 176:192] = both


def spread_kernel(blocks, core, cat, got, cot, mask, mine, other, up_out, inv_out, far):
    degree = jnp.zeros((1, EDGE), F32)
    for r in range(got.shape[0]):
        both = got[r, 176:192].astype(F32)
        degree = degree + both[0:1] * 256.0 + both[1:2]
    inverse = 1.0 / (degree + 1.0)
    inv_out[...] = jnp.broadcast_to(inverse, inv_out.shape)
    upstream = cot[...].astype(F32) * mask[...].astype(F32)
    up_out[...] = upstream.astype(BF)
    scaled = (upstream * inverse).astype(BF)
    mine[...] = jnp.zeros_like(mine)
    far[...] = jnp.zeros_like(far)
    me = core[0]
    for t in range(cat.shape[1] // EDGE):
        block = jnp.maximum(blocks[t], 0)
        product = dot(scaled, cat[:, t * EDGE : (t + 1) * EDGE])
        own = (block & 1) == me
        at = block >> 1
        mine[at] += jnp.where(own, product, 0.0)
        far[at] += jnp.where(own, 0.0, product)
    other[...] = far[...].astype(BF)


def pair_sum_kernel(mine, other, total):
    total[...] = (mine[...] + other[...].astype(F32)).astype(BF)


def plane_sum_kernel(side, got, keep, give):
    total = got[0].astype(F32)
    for j in range(1, got.shape[0]):
        total = total + got[j].astype(F32)
    first = side[0] == 0
    keep[...] = jnp.where(first, total[0:WIDE], total[WIDE:])
    give[...] = jnp.where(first, total[WIDE:], total[0:WIDE])


def gather_one_kernel(blocks, core, own, far, cat, keep, came, send, picked):
    me = core[0]
    n_repl, part = send.shape[0], own.shape[2]
    for t in range(cat.shape[1] // EDGE):
        block = jnp.maximum(blocks[t], 0)
        half = (block >> 1) & 1
        at = block >> 2
        near = (block & 1) == me
        for q in range(n_repl):
            a = own[half * n_repl + q, at]
            b = far[half * n_repl + q, at]
            picked[q * part : (q + 1) * part, t * EDGE : (t + 1) * EDGE] = jnp.where(near, a, b)
    total = dot(picked[...], cat[...], NT)
    terms = keep[...] + came[...]
    for r in range(n_repl):
        send[r, 0:EDGE] = total
        send[r, EDGE:] = terms


def layer_kernel(repl, parts, got, up, inv, features, bias_two, send, base, packed, pad):
    chunk = GRADS // send.shape[0]
    n_repl = got.shape[0]
    both = parts[0]
    for r in range(1, n_repl):
        both = both + parts[r]
    mean = (both[0:EDGE] * inv[0:1]).astype(BF)
    feat = features[...]
    last = lax.broadcasted_iota(jnp.int32, (WIDE, EDGE), 0) == CLASSES
    unit = jnp.where(last, 1.0, 0.0).astype(BF)
    none = jnp.zeros((64, EDGE), BF)

    def before(r):
        bias = dot(got[r, 128:176], unit, TN)[0:64]
        return (dot(got[r, 0:64], feat) + dot(got[r, 64:128], mean)) + bias

    projected = jnp.zeros((WIDE, EDGE), F32)
    skipped = jnp.zeros((WIDE, EDGE), F32)
    for r in range(n_repl):
        pre = before(r)
        hidden = (pre * jax.nn.sigmoid(pre)).astype(BF)
        projected = projected + dot(got[r, 128:176], jnp.concatenate([hidden, none], axis=0))
        skipped = skipped + dot(got[r, 128:176], jnp.concatenate([none, hidden], axis=0))
    projected = projected.astype(BF)
    pad[...] = jnp.zeros_like(pad)
    pad[0:1, 0:CLASSES] = bias_two[...].astype(F32)
    base[...] = skipped + dot(pad[...].astype(BF), jnp.ones((8, EDGE), BF), TN)[0:WIDE]

    pulled = both[EDGE:].astype(BF)
    upstream = up[...]
    mine = repl[0]
    pre = before(mine)
    sigmoid = jax.nn.sigmoid(pre)
    hidden = (pre * sigmoid).astype(BF)
    second = got[mine, 128:176]
    hidden_grad = dot(second, upstream, TN)[64:128] + dot(second, pulled, TN)[0:64]
    pre_grad = (hidden_grad * sigmoid * (1.0 + pre * (1.0 - sigmoid))).astype(BF)
    packed[0:64] = dot(pre_grad, feat, NT)
    packed[64:128] = dot(pre_grad, mean, NT)
    ones = jnp.ones((8, EDGE), BF)
    twice = jnp.concatenate([hidden, hidden], axis=0)
    left = lax.broadcasted_iota(jnp.int32, (WIDE, EDGE), 1) < 64
    grads_two = jnp.where(left, dot(pulled, twice, NT), dot(upstream, twice, NT))
    bias_one = dot(ones, jnp.concatenate([pre_grad, none], axis=0), NT)[0:1]
    packed[128:176] = jnp.where(last, bias_one, grads_two)
    packed[176:184] = dot(ones, jnp.concatenate([upstream, jnp.zeros((EDGE - WIDE, EDGE), BF)], axis=0), NT)
    packed[184:GRADS] = jnp.zeros((GRADS - 184, EDGE), F32)
    for j in range(send.shape[0]):
        send[j, 0:WIDE] = projected
        send[j, WIDE:] = halves(packed[j * chunk : (j + 1) * chunk])


def relay_kernel(got, send):
    sheet = got.shape[0]
    chunk = GRADS // sheet
    total = got[0, WIDE:].astype(F32)
    for j in range(1, sheet):
        total = total + got[j, WIDE:].astype(F32)
    both = halves(total[0:chunk] + total[chunk:])
    for d in range(send.shape[0]):
        for j in range(sheet):
            send[d, j * WIDE : (j + 1) * WIDE] = got[j, 0:WIDE]
        send[d, sheet * WIDE :] = both


def gather_two_kernel(blocks, core, own, far, cat, send, grads, picked):
    me = core[0]
    sheet, chunk = grads.shape[0], grads.shape[1]
    for t in range(cat.shape[1] // EDGE):
        block = jnp.maximum(blocks[t], 0)
        place = block >> 1
        line = place // sheet
        rows = pl.ds(pl.multiple_of((place - line * sheet) * WIDE, 16), WIDE)
        near = (block & 1) == me
        a = own[line, rows]
        b = far[line, rows]
        picked[:, t * EDGE : (t + 1) * EDGE] = jnp.where(near, a, b)
    send[...] = dot(picked[...], cat[...], NT)
    sums = []
    for ref in (own, far):
        both = jnp.zeros((2 * chunk, EDGE), F32)
        for i in range(own.shape[0]):
            both = both + ref[i, sheet * WIDE :].astype(F32)
        sums.append(both[0:chunk] + both[chunk:])
    whole = sums[0] + sums[1]
    for j in range(sheet):
        grads[j] = whole


def scores_kernel(repl, own, first, second, third, base, inv, scores, parts):
    n_repl = parts.shape[0]
    for k, ref in enumerate((own, first, second, third)[:n_repl]):
        at = repl[0] + k
        parts[jnp.where(at >= n_repl, at - n_repl, at)] = ref[...]
    total = parts[0]
    for r in range(1, n_repl):
        total = total + parts[r]
    scores[...] = (base[...] + total * inv[0:1])[0:CLASSES]


def unpack_kernel(grads, self_one, neighbor_one, bias_one, self_two, neighbor_two, bias_two):
    self_one[...] = grads[0:64]
    neighbor_one[...] = grads[64:128]
    neighbor_two[...] = grads[128 : 128 + CLASSES, 0:64]
    self_two[...] = grads[128 : 128 + CLASSES, 64:128]
    bias_one[...] = grads[175:176, 0:64]
    bias_two[...] = grads[176:177, 0:CLASSES]


def per_device(
    sizes,
    features,
    tile_blocks,
    tile_counts,
    train_mask,
    cotangent,
    self_one,
    neighbor_one,
    bias_one,
    self_two,
    neighbor_two,
    bias_two,
):
    n_repl = sizes["yl"]
    plane = sizes["x"] * sizes["z"]
    halves_n = sizes["yh"]
    column = halves_n * n_repl
    tiles = tile_counts.shape[0]
    sheet = sizes["z"] * halves_n
    chunk = GRADS // sheet
    core = lax.axis_index("core").astype(jnp.int32).reshape(1)
    repl = lax.axis_index("yl").astype(jnp.int32).reshape(1)
    side = lax.axis_index("yh").astype(jnp.int32).reshape(1)
    swap = [(0, 1), (1, 0)]

    part = features.shape[0] // n_repl
    quarter = lax.dynamic_slice_in_dim(features, repl[0] * part, part, 0)
    quarters = lax.all_to_all(
        jnp.broadcast_to(quarter[None], (plane, part, EDGE)), PLANE, 0, 0, tiled=True
    )
    order, quarters = lax.optimization_barrier((core, quarters))
    near = lax.all_gather(quarters.reshape(plane * part, EDGE), COLUMN, axis=0, tiled=True)

    send = call(
        prepare_kernel,
        jax.ShapeDtypeStruct((n_repl, 192, EDGE), BF),
        [SMEM] * 2 + [pl.BlockSpec(memory_space=pl.ANY)] * 6,
        [
            pltpu.VMEM((tiles, EDGE, EDGE), jnp.int32),
            pltpu.VMEM((64, EDGE), BF),
            pltpu.VMEM((64, EDGE), BF),
            pltpu.VMEM((CLASSES, 64), BF),
            pltpu.VMEM((CLASSES, 64), BF),
            pltpu.VMEM((1, 64), BF),
            pltpu.VMEM((WIDE, EDGE), F32),
            pltpu.SemaphoreType.DMA((8,)),
            pltpu.SemaphoreType.DMA((5,)),
        ],
        60,
    )(
        tile_blocks,
        order,
        tile_counts,
        self_one.T,
        neighbor_one.T,
        neighbor_two.T,
        self_two.T,
        bias_one[None, :],
    )
    got = lax.all_to_all(send, "yl", 0, 0, tiled=True)
    cat = call(lay_kernel, jax.ShapeDtypeStruct((EDGE, tiles * EDGE), BF), [SMEM, VMEM])(
        tile_blocks, tile_counts
    )

    cot = jnp.pad(cotangent, ((0, WIDE - CLASSES), (0, 0)))
    mine, other, up, inv = call(
        spread_kernel,
        (
            jax.ShapeDtypeStruct((plane * halves_n, WIDE, EDGE), F32),
            jax.ShapeDtypeStruct((plane * halves_n, WIDE, EDGE), BF),
            jax.ShapeDtypeStruct((WIDE, EDGE), BF),
            jax.ShapeDtypeStruct((8, EDGE), F32),
        ),
        [SMEM, SMEM] + [VMEM] * 4,
        [pltpu.VMEM((plane * halves_n, WIDE, EDGE), F32)],
    )(tile_blocks, core, cat, got, cot, train_mask[None, :])
    back = call(
        pair_sum_kernel,
        jax.ShapeDtypeStruct((plane * halves_n, WIDE, EDGE), BF),
        [VMEM] * 2,
    )(mine, lax.ppermute(other, "core", swap))
    back = lax.all_to_all(back.reshape(plane, halves_n * WIDE, EDGE), PLANE, 0, 0, tiled=True)
    near, back = lax.optimization_barrier((near, back))
    far = lax.ppermute(near, "core", swap)
    half = jax.ShapeDtypeStruct((WIDE, EDGE), F32)
    keep, give = call(plane_sum_kernel, (half, half), [SMEM, VMEM])(side, back)
    came = lax.ppermute(give, "yh", swap)

    shape = (column, plane, part, EDGE)
    parts = call(
        gather_one_kernel,
        jax.ShapeDtypeStruct((n_repl, EDGE + WIDE, EDGE), F32),
        [SMEM, SMEM] + [VMEM] * 5,
        [pltpu.VMEM((EDGE, tiles * EDGE), BF)],
    )(tile_blocks, core, near.reshape(shape), far.reshape(shape), cat, keep, came)
    parts = lax.all_to_all(parts, "yl", 0, 0, tiled=True)

    send, base = call(
        layer_kernel,
        (
            jax.ShapeDtypeStruct((sheet, WIDE + 2 * chunk, EDGE), BF),
            jax.ShapeDtypeStruct((WIDE, EDGE), F32),
        ),
        [SMEM] + [VMEM] * 6,
        [pltpu.VMEM((GRADS, EDGE), F32), pltpu.VMEM((8, EDGE), F32)],
    )(repl, parts, got, up, inv, features, bias_two[None, :])
    relay = lax.all_to_all(send, SHEET, 0, 0, tiled=True)
    relay = call(
        relay_kernel,
        jax.ShapeDtypeStruct((sizes["x"], sheet * WIDE + 2 * chunk, EDGE), BF),
        [VMEM],
    )(relay)
    near_two = lax.all_to_all(relay, "x", 0, 0, tiled=True)
    far_two = lax.ppermute(near_two, "core", swap)
    second, grads = call(
        gather_two_kernel,
        (
            jax.ShapeDtypeStruct((WIDE, EDGE), F32),
            jax.ShapeDtypeStruct((sheet, chunk, EDGE), F32),
        ),
        [SMEM] * 2 + [VMEM] * 3,
        [pltpu.VMEM((WIDE, tiles * EDGE), BF)],
    )(tile_blocks, core, near_two, far_two, cat)
    others = [
        lax.ppermute(second, "yl", [((i + k) % n_repl, i) for i in range(n_repl)])
        for k in range(1, n_repl)
    ]
    grads = lax.all_to_all(grads, SHEET, 0, 0, tiled=True).reshape(GRADS, EDGE)
    others = others + [second] * (3 - len(others))
    scores = call(
        scores_kernel,
        jax.ShapeDtypeStruct((CLASSES, EDGE), F32),
        [SMEM] + [VMEM] * 6,
        [pltpu.VMEM((n_repl, WIDE, EDGE), F32)],
    )(repl, second, *others, base, inv)
    one = jax.ShapeDtypeStruct((64, EDGE), F32)
    two = jax.ShapeDtypeStruct((CLASSES, 64), F32)
    self_one, neighbor_one, bias_one, self_two, neighbor_two, bias_two = call(
        unpack_kernel,
        (
            one,
            one,
            jax.ShapeDtypeStruct((1, 64), F32),
            two,
            two,
            jax.ShapeDtypeStruct((1, CLASSES), F32),
        ),
        [VMEM],
    )(grads)
    return (
        scores,
        self_one.T,
        neighbor_one.T,
        bias_one[0],
        self_two.T,
        neighbor_two.T,
        bias_two[0],
    )


def solution(mesh):
    sizes = {"x": 4, "z": 8, "yh": 2, "core": 2, "yl": 4}
    fine = Mesh(mesh.devices.reshape(tuple(sizes.values())), tuple(sizes))
    return sharded(fine, sizes)


def sharded(fine, sizes):
    both = ROWS + ("yl",)
    return jax.shard_map(
        functools.partial(per_device, sizes),
        mesh=fine,
        in_specs=(
            P(None, ROWS),
            P(both),
            P(both, None, None),
            P(ROWS),
            P(None, ROWS),
            P(None, "yl"),
            P(None, "yl"),
            P("yl"),
            P("yl", None),
            P("yl", None),
            P(),
        ),
        out_specs=(
            P(None, ROWS),
            P(None, "yl"),
            P(None, "yl"),
            P("yl"),
            P("yl", None),
            P("yl", None),
            P(),
        ),
        check_vma=False,
    )
```

```python
import functools

import jax
import jax.numpy as jnp
from jax import lax
from jax.experimental import pallas as pl
from jax.experimental.pallas import tpu as pltpu
from jax.sharding import Mesh, PartitionSpec as P

BF = jnp.bfloat16
F32 = jnp.float32
CLASSES = 47
WIDE = 48
EDGE = 128
ROWS = ("x", "z", "yh", "core")
PLANE = ("x", "z")
COLUMN = ("yh", "yl")
SHEET = ("z", "yh")
GRADS = 256
VMEM = pl.BlockSpec(memory_space=pltpu.VMEM)
SMEM = pl.BlockSpec(memory_space=pltpu.SMEM)
NT = (((1,), (1,)), ((), ()))
TN = (((0,), (0,)), ((), ()))


def dot(a, b, dims=(((1,), (0,)), ((), ()))):
    return lax.dot_general(a, b, dims, preferred_element_type=F32)


def call(body, outs, in_specs, scratch=(), room=40):
    return pl.pallas_call(
        body,
        out_shape=outs,
        in_specs=in_specs,
        out_specs=jax.tree.map(lambda _: VMEM, outs),
        scratch_shapes=list(scratch),
        compiler_params=pltpu.CompilerParams(vmem_limit_bytes=room * 1024 * 1024),
    )


def halves(value):
    high = value.astype(BF).astype(F32)
    return jnp.concatenate([high, value - high], axis=0).astype(BF)


def quarter_kernel(repl, features, send):
    rows = send.shape[1]
    part = features[pl.ds(pl.multiple_of(repl[0] * rows, 16), rows)]
    for j in range(send.shape[0]):
        send[j] = part


def lay_kernel(blocks, counts, cat):
    for t in range(counts.shape[0]):
        tile = jnp.where(blocks[t] >= 0, counts[t], 0).astype(F32)
        cat[:, t * EDGE : (t + 1) * EDGE] = tile.astype(BF)


def prepare_kernel(blocks, counts, one, two, three, four, five, send, *scratch):
    held, self_one, neighbor_one, neighbor_two, self_two, bias, second, done, ready = scratch
    steps = done.shape[0]
    per = held.shape[0] // steps
    copies = [
        pltpu.make_async_copy(
            counts.at[pl.ds(i * per, per)], held.at[pl.ds(i * per, per)], done.at[i]
        )
        for i in range(steps)
    ]
    pairs = zip((one, two, three, four, five), scratch[1:6])
    weights = [pltpu.make_async_copy(a, b, ready.at[i]) for i, (a, b) in enumerate(pairs)]
    for copy in copies + weights:
        copy.start()
    running = jnp.zeros((EDGE, EDGE), jnp.int32)
    for i, copy in enumerate(copies):
        copy.wait()
        for t in range(i * per, (i + 1) * per):
            running = running + jnp.where(blocks[t] >= 0, held[t], 0)
    for copy in weights:
        copy.wait()
    whole = dot(jnp.ones((8, EDGE), BF), running.astype(F32).astype(BF), NT)[0:1]
    high = jnp.floor(whole * (1.0 / 256.0))
    low = whole - high * 256.0
    row = lax.broadcasted_iota(jnp.int32, (16, EDGE), 0)
    both = jnp.where(row == 0, high, jnp.where(row == 1, low, 0.0)).astype(BF)
    second[...] = jnp.zeros_like(second)
    second[0:CLASSES, 0:64] = neighbor_two[...].astype(F32)
    second[CLASSES:WIDE, 0:64] = bias[...].astype(F32)
    second[0:CLASSES, 64:128] = self_two[...].astype(F32)
    layer_two = second[...].astype(BF)
    for r in range(send.shape[0]):
        send[r, 0:64] = self_one[...]
        send[r, 64:128] = neighbor_one[...]
        send[r, 128:176] = layer_two
        send[r, 176:192] = both


def spread_kernel(blocks, core, cat, got, cot, mask, mine, other, up_out, inv_out, far):
    degree = jnp.zeros((1, EDGE), F32)
    for r in range(got.shape[0]):
        both = got[r, 176:192].astype(F32)
        degree = degree + both[0:1] * 256.0 + both[1:2]
    inverse = 1.0 / (degree + 1.0)
    inv_out[...] = jnp.broadcast_to(inverse, inv_out.shape)
    upstream = cot[...].astype(F32) * mask[...].astype(F32)
    up_out[...] = upstream.astype(BF)
    scaled = (upstream * inverse).astype(BF)
    mine[...] = jnp.zeros_like(mine)
    far[...] = jnp.zeros_like(far)
    me = core[0]
    for t in range(cat.shape[1] // EDGE):
        block = jnp.maximum(blocks[t], 0)
        product = dot(scaled, cat[:, t * EDGE : (t + 1) * EDGE])
        own = (block & 1) == me
        at = block >> 1
        mine[at] += jnp.where(own, product, 0.0)
        far[at] += jnp.where(own, 0.0, product)
    other[...] = far[...].astype(BF)


def pair_sum_kernel(mine, other, total):
    total[...] = (mine[...] + other[...].astype(F32)).astype(BF)


def plane_sum_kernel(side, got, keep, give):
    total = got[0].astype(F32)
    for j in range(1, got.shape[0]):
        total = total + got[j].astype(F32)
    first = side[0] == 0
    keep[...] = jnp.where(first, total[0:WIDE], total[WIDE:])
    give[...] = jnp.where(first, total[WIDE:], total[0:WIDE])


def gather_one_kernel(blocks, core, own, far, cat, total, picked):
    me = core[0]
    part = own.shape[2]
    n_repl = EDGE // part
    for t in range(cat.shape[1] // EDGE):
        block = jnp.maximum(blocks[t], 0)
        half = (block >> 1) & 1
        at = block >> 2
        near = (block & 1) == me
        for q in range(n_repl):
            a = own[half * n_repl + q, at]
            b = far[half * n_repl + q, at]
            picked[q * part : (q + 1) * part, t * EDGE : (t + 1) * EDGE] = jnp.where(near, a, b)
    total[...] = dot(picked[...], cat[...], NT)


def mix_kernel(total, keep, came, send):
    part = halves(total[...])
    terms = (keep[...] + came[...]).astype(BF)
    for r in range(send.shape[0]):
        send[r, 0 : 2 * EDGE] = part
        send[r, 2 * EDGE :] = terms


def layer_kernel(repl, parts, got, up, inv, features, bias_two, send, base, packed, pad):
    chunk = GRADS // send.shape[0]
    n_repl = got.shape[0]
    both = parts[0].astype(F32)
    for r in range(1, n_repl):
        both = both + parts[r].astype(F32)
    mean = ((both[0:EDGE] + both[EDGE : 2 * EDGE]) * inv[0:1]).astype(BF)
    feat = features[...]
    last = lax.broadcasted_iota(jnp.int32, (WIDE, EDGE), 0) == CLASSES
    unit = jnp.where(last, 1.0, 0.0).astype(BF)
    none = jnp.zeros((64, EDGE), BF)

    def before(r):
        bias = dot(got[r, 128:176], unit, TN)[0:64]
        return (dot(got[r, 0:64], feat) + dot(got[r, 64:128], mean)) + bias

    projected = jnp.zeros((WIDE, EDGE), F32)
    skipped = jnp.zeros((WIDE, EDGE), F32)
    for r in range(n_repl):
        pre = before(r)
        hidden = (pre * jax.nn.sigmoid(pre)).astype(BF)
        projected = projected + dot(got[r, 128:176], jnp.concatenate([hidden, none], axis=0))
        skipped = skipped + dot(got[r, 128:176], jnp.concatenate([none, hidden], axis=0))
    projected = projected.astype(BF)
    pad[...] = jnp.zeros_like(pad)
    pad[0:1, 0:CLASSES] = bias_two[...].astype(F32)
    base[...] = skipped + dot(pad[...].astype(BF), jnp.ones((8, EDGE), BF), TN)[0:WIDE]

    pulled = both[2 * EDGE :].astype(BF)
    upstream = up[...]
    mine = repl[0]
    pre = before(mine)
    sigmoid = jax.nn.sigmoid(pre)
    hidden = (pre * sigmoid).astype(BF)
    second = got[mine, 128:176]
    hidden_grad = dot(second, upstream, TN)[64:128] + dot(second, pulled, TN)[0:64]
    pre_grad = (hidden_grad * sigmoid * (1.0 + pre * (1.0 - sigmoid))).astype(BF)
    packed[0:64] = dot(pre_grad, feat, NT)
    packed[64:128] = dot(pre_grad, mean, NT)
    ones = jnp.ones((8, EDGE), BF)
    twice = jnp.concatenate([hidden, hidden], axis=0)
    left = lax.broadcasted_iota(jnp.int32, (WIDE, EDGE), 1) < 64
    grads_two = jnp.where(left, dot(pulled, twice, NT), dot(upstream, twice, NT))
    bias_one = dot(ones, jnp.concatenate([pre_grad, none], axis=0), NT)[0:1]
    packed[128:176] = jnp.where(last, bias_one, grads_two)
    packed[176:184] = dot(ones, jnp.concatenate([upstream, jnp.zeros((EDGE - WIDE, EDGE), BF)], axis=0), NT)
    packed[184:GRADS] = jnp.zeros((GRADS - 184, EDGE), F32)
    for j in range(send.shape[0]):
        send[j, 0:WIDE] = projected
        send[j, WIDE:] = halves(packed[j * chunk : (j + 1) * chunk])


def relay_kernel(got, send):
    sheet = got.shape[0]
    chunk = GRADS // sheet
    total = got[0, WIDE:].astype(F32)
    for j in range(1, sheet):
        total = total + got[j, WIDE:].astype(F32)
    both = halves(total[0:chunk] + total[chunk:])
    for d in range(send.shape[0]):
        for j in range(sheet):
            send[d, j * WIDE : (j + 1) * WIDE] = got[j, 0:WIDE]
        send[d, sheet * WIDE :] = both


def gather_two_kernel(sheet, blocks, core, own, far, cat, send, picked):
    me = core[0]
    for t in range(cat.shape[1] // EDGE):
        block = jnp.maximum(blocks[t], 0)
        place = block >> 1
        line = place // sheet
        rows = pl.ds(pl.multiple_of((place - line * sheet) * WIDE, 16), WIDE)
        near = (block & 1) == me
        a = own[line, rows]
        b = far[line, rows]
        picked[:, t * EDGE : (t + 1) * EDGE] = jnp.where(near, a, b)
    send[...] = dot(picked[...], cat[...], NT)


def chunk_sum_kernel(got, grads):
    chunk = grads.shape[1]
    both = got[0].astype(F32)
    for i in range(1, got.shape[0]):
        both = both + got[i].astype(F32)
    total = both[0:chunk] + both[chunk:]
    for j in range(grads.shape[0]):
        grads[j] = total


def scores_kernel(repl, own, first, second, third, base, inv, scores, parts):
    n_repl = parts.shape[0]
    for k, ref in enumerate((own, first, second, third)[:n_repl]):
        at = repl[0] + k
        parts[jnp.where(at >= n_repl, at - n_repl, at)] = ref[...]
    total = parts[0]
    for r in range(1, n_repl):
        total = total + parts[r]
    scores[...] = (base[...] + total * inv[0:1])[0:CLASSES]


def unpack_kernel(
    got, self_one, neighbor_one, bias_one, self_two, neighbor_two, bias_two, grads
):
    chunk = got.shape[1]
    for j in range(got.shape[0] // 2):
        grads[j * chunk : (j + 1) * chunk] = got[2 * j] + got[2 * j + 1]
    self_one[...] = grads[0:64]
    neighbor_one[...] = grads[64:128]
    neighbor_two[...] = grads[128 : 128 + CLASSES, 0:64]
    self_two[...] = grads[128 : 128 + CLASSES, 64:128]
    bias_one[...] = grads[175:176, 0:64]
    bias_two[...] = grads[176:177, 0:CLASSES]


def per_device(
    sizes,
    features,
    tile_blocks,
    tile_counts,
    train_mask,
    cotangent,
    self_one,
    neighbor_one,
    bias_one,
    self_two,
    neighbor_two,
    bias_two,
):
    n_repl = sizes["yl"]
    plane = sizes["x"] * sizes["z"]
    halves_n = sizes["yh"]
    column = halves_n * n_repl
    tiles = tile_counts.shape[0]
    sheet = sizes["z"] * halves_n
    chunk = GRADS // sheet
    core = lax.axis_index("core").astype(jnp.int32).reshape(1)
    repl = lax.axis_index("yl").astype(jnp.int32).reshape(1)
    side = lax.axis_index("yh").astype(jnp.int32).reshape(1)
    swap = [(0, 1), (1, 0)]

    part = features.shape[0] // n_repl
    quarters = call(quarter_kernel, jax.ShapeDtypeStruct((plane, part, EDGE), BF), [SMEM, VMEM])(
        repl, features
    )
    quarters = lax.all_to_all(quarters, PLANE, 0, 0, tiled=True)

    send = call(
        prepare_kernel,
        jax.ShapeDtypeStruct((n_repl, 192, EDGE), BF),
        [SMEM] + [pl.BlockSpec(memory_space=pl.ANY)] * 6,
        [
            pltpu.VMEM((tiles, EDGE, EDGE), jnp.int32),
            pltpu.VMEM((64, EDGE), BF),
            pltpu.VMEM((64, EDGE), BF),
            pltpu.VMEM((CLASSES, 64), BF),
            pltpu.VMEM((CLASSES, 64), BF),
            pltpu.VMEM((1, 64), BF),
            pltpu.VMEM((WIDE, EDGE), F32),
            pltpu.SemaphoreType.DMA((8,)),
            pltpu.SemaphoreType.DMA((5,)),
        ],
        60,
    )(
        tile_blocks,
        tile_counts,
        self_one.T,
        neighbor_one.T,
        neighbor_two.T,
        self_two.T,
        bias_one[None, :],
    )
    quarters, send = lax.optimization_barrier((quarters, send))
    near = lax.all_gather(quarters.reshape(plane * part, EDGE), COLUMN, axis=0, tiled=True)
    got = lax.all_to_all(send, "yl", 0, 0, tiled=True)
    cat = call(lay_kernel, jax.ShapeDtypeStruct((EDGE, tiles * EDGE), BF), [SMEM, VMEM])(
        tile_blocks, tile_counts
    )

    cot = jnp.pad(cotangent, ((0, WIDE - CLASSES), (0, 0)))
    mine, other, up, inv = call(
        spread_kernel,
        (
            jax.ShapeDtypeStruct((plane * halves_n, WIDE, EDGE), F32),
            jax.ShapeDtypeStruct((plane * halves_n, WIDE, EDGE), BF),
            jax.ShapeDtypeStruct((WIDE, EDGE), BF),
            jax.ShapeDtypeStruct((8, EDGE), F32),
        ),
        [SMEM, SMEM] + [VMEM] * 4,
        [pltpu.VMEM((plane * halves_n, WIDE, EDGE), F32)],
    )(tile_blocks, core, cat, got, cot, train_mask[None, :])
    back = call(
        pair_sum_kernel,
        jax.ShapeDtypeStruct((plane * halves_n, WIDE, EDGE), BF),
        [VMEM] * 2,
    )(mine, lax.ppermute(other, "core", swap))
    back = lax.all_to_all(back.reshape(plane, halves_n * WIDE, EDGE), PLANE, 0, 0, tiled=True)
    near, back = lax.optimization_barrier((near, back))
    far = lax.ppermute(near, "core", swap)
    half = jax.ShapeDtypeStruct((WIDE, EDGE), F32)
    keep, give = call(plane_sum_kernel, (half, half), [SMEM, VMEM])(side, back)
    came = lax.ppermute(give, "yh", swap)

    shape = (column, plane, part, EDGE)
    total = call(
        gather_one_kernel,
        jax.ShapeDtypeStruct((EDGE, EDGE), F32),
        [SMEM, SMEM] + [VMEM] * 3,
        [pltpu.VMEM((EDGE, tiles * EDGE), BF)],
    )(tile_blocks, core, near.reshape(shape), far.reshape(shape), cat)
    parts = call(
        mix_kernel, jax.ShapeDtypeStruct((n_repl, 2 * EDGE + WIDE, EDGE), BF), [VMEM] * 3
    )(total, keep, came)
    parts = lax.all_to_all(parts, "yl", 0, 0, tiled=True)

    send, base = call(
        layer_kernel,
        (
            jax.ShapeDtypeStruct((sheet, WIDE + 2 * chunk, EDGE), BF),
            jax.ShapeDtypeStruct((WIDE, EDGE), F32),
        ),
        [SMEM] + [VMEM] * 6,
        [pltpu.VMEM((GRADS, EDGE), F32), pltpu.VMEM((8, EDGE), F32)],
    )(repl, parts, got, up, inv, features, bias_two[None, :])
    relay = lax.all_to_all(send, SHEET, 0, 0, tiled=True)
    relay = call(
        relay_kernel,
        jax.ShapeDtypeStruct((sizes["x"], sheet * WIDE + 2 * chunk, EDGE), BF),
        [VMEM],
    )(relay)
    near_two = lax.all_to_all(relay, "x", 0, 0, tiled=True)
    far_two = lax.ppermute(near_two, "core", swap)
    grads = call(
        chunk_sum_kernel, jax.ShapeDtypeStruct((2 * sheet, chunk, EDGE), F32), [VMEM]
    )(near_two[:, sheet * WIDE :])
    grads = lax.all_to_all(grads, SHEET + ("core",), 0, 0, tiled=True)
    second = call(
        functools.partial(gather_two_kernel, sheet),
        jax.ShapeDtypeStruct((WIDE, EDGE), F32),
        [SMEM] * 2 + [VMEM] * 3,
        [pltpu.VMEM((WIDE, tiles * EDGE), BF)],
    )(tile_blocks, core, near_two, far_two, cat)
    others = [
        lax.ppermute(second, "yl", [((i + k) % n_repl, i) for i in range(n_repl)])
        for k in range(1, n_repl)
    ]
    others = others + [second] * (3 - len(others))
    scores = call(
        scores_kernel,
        jax.ShapeDtypeStruct((CLASSES, EDGE), F32),
        [SMEM] + [VMEM] * 6,
        [pltpu.VMEM((n_repl, WIDE, EDGE), F32)],
    )(repl, second, *others, base, inv)
    one = jax.ShapeDtypeStruct((64, EDGE), F32)
    two = jax.ShapeDtypeStruct((CLASSES, 64), F32)
    self_one, neighbor_one, bias_one, self_two, neighbor_two, bias_two = call(
        unpack_kernel,
        (
            one,
            one,
            jax.ShapeDtypeStruct((1, 64), F32),
            two,
            two,
            jax.ShapeDtypeStruct((1, CLASSES), F32),
        ),
        [VMEM],
        [pltpu.VMEM((GRADS, EDGE), F32)],
    )(grads)
    return (
        scores,
        self_one.T,
        neighbor_one.T,
        bias_one[0],
        self_two.T,
        neighbor_two.T,
        bias_two[0],
    )


def solution(mesh):
    sizes = {"x": 4, "z": 8, "yh": 2, "core": 2, "yl": 4}
    fine = Mesh(mesh.devices.reshape(tuple(sizes.values())), tuple(sizes))
    return sharded(fine, sizes)


def sharded(fine, sizes):
    both = ROWS + ("yl",)
    return jax.shard_map(
        functools.partial(per_device, sizes),
        mesh=fine,
        in_specs=(
            P(None, ROWS),
            P(both),
            P(both, None, None),
            P(ROWS),
            P(None, ROWS),
            P(None, "yl"),
            P(None, "yl"),
            P("yl"),
            P("yl", None),
            P("yl", None),
            P(),
        ),
        out_specs=(
            P(None, ROWS),
            P(None, "yl"),
            P(None, "yl"),
            P("yl"),
            P("yl", None),
            P("yl", None),
            P(),
        ),
        check_vma=False,
    )
```

```python
import functools

import jax
import jax.numpy as jnp
from jax import lax
from jax.experimental import pallas as pl
from jax.experimental.pallas import tpu as pltpu
from jax.sharding import Mesh, PartitionSpec as P

BF = jnp.bfloat16
F32 = jnp.float32
CLASSES = 47
WIDE = 48
EDGE = 128
ROWS = ("x", "z", "yh", "core")
PLANE = ("x", "z")
COLUMN = ("yh", "yl")
SHEET = ("z", "yh")
GRADS = 256
VMEM = pl.BlockSpec(memory_space=pltpu.VMEM)
SMEM = pl.BlockSpec(memory_space=pltpu.SMEM)
NT = (((1,), (1,)), ((), ()))
TN = (((0,), (0,)), ((), ()))


def dot(a, b, dims=(((1,), (0,)), ((), ()))):
    return lax.dot_general(a, b, dims, preferred_element_type=F32)


def call(body, outs, in_specs, scratch=(), room=40):
    return pl.pallas_call(
        body,
        out_shape=outs,
        in_specs=in_specs,
        out_specs=jax.tree.map(lambda _: VMEM, outs),
        scratch_shapes=list(scratch),
        compiler_params=pltpu.CompilerParams(vmem_limit_bytes=room * 1024 * 1024),
    )


def halves(value):
    high = value.astype(BF).astype(F32)
    return jnp.concatenate([high, value - high], axis=0).astype(BF)


def quarter_kernel(repl, features, send):
    rows = send.shape[1]
    part = features[pl.ds(pl.multiple_of(repl[0] * rows, 16), rows)]
    for j in range(send.shape[0]):
        send[j] = part


def lay_kernel(blocks, counts, cat):
    for t in range(counts.shape[0]):
        tile = jnp.where(blocks[t] >= 0, counts[t], 0).astype(F32)
        cat[:, t * EDGE : (t + 1) * EDGE] = tile.astype(BF)


def prepare_kernel(blocks, counts, one, two, three, four, five, send, *scratch):
    held, self_one, neighbor_one, neighbor_two, self_two, bias, second, done, ready = scratch
    steps = done.shape[0]
    per = held.shape[0] // steps
    copies = [
        pltpu.make_async_copy(
            counts.at[pl.ds(i * per, per)], held.at[pl.ds(i * per, per)], done.at[i]
        )
        for i in range(steps)
    ]
    pairs = zip((one, two, three, four, five), scratch[1:6])
    weights = [pltpu.make_async_copy(a, b, ready.at[i]) for i, (a, b) in enumerate(pairs)]
    for copy in copies + weights:
        copy.start()
    running = jnp.zeros((EDGE, EDGE), jnp.int32)
    for i, copy in enumerate(copies):
        copy.wait()
        for t in range(i * per, (i + 1) * per):
            running = running + jnp.where(blocks[t] >= 0, held[t], 0)
    for copy in weights:
        copy.wait()
    whole = dot(jnp.ones((8, EDGE), BF), running.astype(F32).astype(BF), NT)[0:1]
    high = jnp.floor(whole * (1.0 / 256.0))
    low = whole - high * 256.0
    row = lax.broadcasted_iota(jnp.int32, (16, EDGE), 0)
    both = jnp.where(row == 0, high, jnp.where(row == 1, low, 0.0)).astype(BF)
    second[...] = jnp.zeros_like(second)
    second[0:CLASSES, 0:64] = neighbor_two[...].astype(F32)
    second[CLASSES:WIDE, 0:64] = bias[...].astype(F32)
    second[0:CLASSES, 64:128] = self_two[...].astype(F32)
    layer_two = second[...].astype(BF)
    for r in range(send.shape[0]):
        send[r, 0:64] = self_one[...]
        send[r, 64:128] = neighbor_one[...]
        send[r, 128:176] = layer_two
        send[r, 176:192] = both


def spread_kernel(blocks, core, cat, got, cot, mask, mine, other, up_out, inv_out, far):
    degree = jnp.zeros((1, EDGE), F32)
    for r in range(got.shape[0]):
        both = got[r, 176:192].astype(F32)
        degree = degree + both[0:1] * 256.0 + both[1:2]
    inverse = 1.0 / (degree + 1.0)
    inv_out[...] = jnp.broadcast_to(inverse, inv_out.shape)
    upstream = cot[...].astype(F32) * mask[...].astype(F32)
    up_out[...] = upstream.astype(BF)
    scaled = (upstream * inverse).astype(BF)
    mine[...] = jnp.zeros_like(mine)
    far[...] = jnp.zeros_like(far)
    me = core[0]
    for t in range(cat.shape[1] // EDGE):
        block = jnp.maximum(blocks[t], 0)
        product = dot(scaled, cat[:, t * EDGE : (t + 1) * EDGE])
        own = (block & 1) == me
        at = block >> 1
        mine[at] += jnp.where(own, product, 0.0)
        far[at] += jnp.where(own, 0.0, product)
    other[...] = far[...].astype(BF)


def pair_sum_kernel(mine, other, total):
    total[...] = (mine[...] + other[...].astype(F32)).astype(BF)


def plane_sum_kernel(side, got, keep, give):
    total = got[0].astype(F32)
    for j in range(1, got.shape[0]):
        total = total + got[j].astype(F32)
    first = side[0] == 0
    keep[...] = jnp.where(first, total[0:WIDE], total[WIDE:])
    give[...] = jnp.where(first, total[WIDE:], total[0:WIDE])


def gather_one_kernel(blocks, core, own, far, cat, total, picked):
    me = core[0]
    part = own.shape[2]
    n_repl = EDGE // part
    for t in range(cat.shape[1] // EDGE):
        block = jnp.maximum(blocks[t], 0)
        half = (block >> 1) & 1
        at = block >> 2
        near = (block & 1) == me
        for q in range(n_repl):
            a = own[half * n_repl + q, at]
            b = far[half * n_repl + q, at]
            picked[q * part : (q + 1) * part, t * EDGE : (t + 1) * EDGE] = jnp.where(near, a, b)
    total[...] = dot(picked[...], cat[...], NT)


def mix_kernel(total, keep, came, send):
    part = total[...].astype(BF)
    terms = (keep[...] + came[...]).astype(BF)
    for r in range(send.shape[0]):
        send[r, 0:EDGE] = part
        send[r, EDGE:] = terms


def layer_kernel(repl, parts, got, up, inv, features, bias_two, send, base, packed, pad):
    chunk = GRADS // send.shape[0]
    n_repl = got.shape[0]
    both = parts[0].astype(F32)
    for r in range(1, n_repl):
        both = both + parts[r].astype(F32)
    mean = (both[0:EDGE] * inv[0:1]).astype(BF)
    feat = features[...]
    last = lax.broadcasted_iota(jnp.int32, (WIDE, EDGE), 0) == CLASSES
    unit = jnp.where(last, 1.0, 0.0).astype(BF)
    none = jnp.zeros((64, EDGE), BF)

    def before(r):
        bias = dot(got[r, 128:176], unit, TN)[0:64]
        return (dot(got[r, 0:64], feat) + dot(got[r, 64:128], mean)) + bias

    projected = jnp.zeros((WIDE, EDGE), F32)
    skipped = jnp.zeros((WIDE, EDGE), F32)
    for r in range(n_repl):
        pre = before(r)
        hidden = (pre * jax.nn.sigmoid(pre)).astype(BF)
        projected = projected + dot(got[r, 128:176], jnp.concatenate([hidden, none], axis=0))
        skipped = skipped + dot(got[r, 128:176], jnp.concatenate([none, hidden], axis=0))
    projected = projected.astype(BF)
    pad[...] = jnp.zeros_like(pad)
    pad[0:1, 0:CLASSES] = bias_two[...].astype(F32)
    base[...] = skipped + dot(pad[...].astype(BF), jnp.ones((8, EDGE), BF), TN)[0:WIDE]

    pulled = both[EDGE:].astype(BF)
    upstream = up[...]
    mine = repl[0]
    pre = before(mine)
    sigmoid = jax.nn.sigmoid(pre)
    hidden = (pre * sigmoid).astype(BF)
    second = got[mine, 128:176]
    hidden_grad = dot(second, upstream, TN)[64:128] + dot(second, pulled, TN)[0:64]
    pre_grad = (hidden_grad * sigmoid * (1.0 + pre * (1.0 - sigmoid))).astype(BF)
    packed[0:64] = dot(pre_grad, feat, NT)
    packed[64:128] = dot(pre_grad, mean, NT)
    ones = jnp.ones((8, EDGE), BF)
    twice = jnp.concatenate([hidden, hidden], axis=0)
    left = lax.broadcasted_iota(jnp.int32, (WIDE, EDGE), 1) < 64
    grads_two = jnp.where(left, dot(pulled, twice, NT), dot(upstream, twice, NT))
    bias_one = dot(ones, jnp.concatenate([pre_grad, none], axis=0), NT)[0:1]
    packed[128:176] = jnp.where(last, bias_one, grads_two)
    packed[176:184] = dot(ones, jnp.concatenate([upstream, jnp.zeros((EDGE - WIDE, EDGE), BF)], axis=0), NT)
    packed[184:GRADS] = jnp.zeros((GRADS - 184, EDGE), F32)
    for j in range(send.shape[0]):
        send[j, 0:WIDE] = projected
        send[j, WIDE:] = halves(packed[j * chunk : (j + 1) * chunk])


def relay_kernel(got, send):
    sheet = got.shape[0]
    chunk = GRADS // sheet
    total = got[0, WIDE:].astype(F32)
    for j in range(1, sheet):
        total = total + got[j, WIDE:].astype(F32)
    both = halves(total[0:chunk] + total[chunk:])
    for d in range(send.shape[0]):
        for j in range(sheet):
            send[d, j * WIDE : (j + 1) * WIDE] = got[j, 0:WIDE]
        send[d, sheet * WIDE :] = both


def gather_two_kernel(sheet, blocks, core, own, far, cat, send, picked):
    me = core[0]
    for t in range(cat.shape[1] // EDGE):
        block = jnp.maximum(blocks[t], 0)
        place = block >> 1
        line = place // sheet
        rows = pl.ds(pl.multiple_of((place - line * sheet) * WIDE, 16), WIDE)
        near = (block & 1) == me
        a = own[line, rows]
        b = far[line, rows]
        picked[:, t * EDGE : (t + 1) * EDGE] = jnp.where(near, a, b)
    send[...] = dot(picked[...], cat[...], NT)


def chunk_sum_kernel(got, grads):
    chunk = grads.shape[1]
    both = got[0].astype(F32)
    for i in range(1, got.shape[0]):
        both = both + got[i].astype(F32)
    total = both[0:chunk] + both[chunk:]
    for j in range(grads.shape[0]):
        grads[j] = total


def scores_kernel(repl, own, first, second, third, base, inv, scores, parts):
    n_repl = parts.shape[0]
    for k, ref in enumerate((own, first, second, third)[:n_repl]):
        at = repl[0] + k
        parts[jnp.where(at >= n_repl, at - n_repl, at)] = ref[...]
    total = parts[0]
    for r in range(1, n_repl):
        total = total + parts[r]
    scores[...] = (base[...] + total * inv[0:1])[0:CLASSES]


def unpack_kernel(
    got, self_one, neighbor_one, bias_one, self_two, neighbor_two, bias_two, grads
):
    chunk = got.shape[1]
    for j in range(got.shape[0] // 2):
        grads[j * chunk : (j + 1) * chunk] = got[2 * j] + got[2 * j + 1]
    self_one[...] = grads[0:64]
    neighbor_one[...] = grads[64:128]
    neighbor_two[...] = grads[128 : 128 + CLASSES, 0:64]
    self_two[...] = grads[128 : 128 + CLASSES, 64:128]
    bias_one[...] = grads[175:176, 0:64]
    bias_two[...] = grads[176:177, 0:CLASSES]


def per_device(
    sizes,
    features,
    tile_blocks,
    tile_counts,
    train_mask,
    cotangent,
    self_one,
    neighbor_one,
    bias_one,
    self_two,
    neighbor_two,
    bias_two,
):
    n_repl = sizes["yl"]
    plane = sizes["x"] * sizes["z"]
    halves_n = sizes["yh"]
    column = halves_n * n_repl
    tiles = tile_counts.shape[0]
    sheet = sizes["z"] * halves_n
    chunk = GRADS // sheet
    core = lax.axis_index("core").astype(jnp.int32).reshape(1)
    repl = lax.axis_index("yl").astype(jnp.int32).reshape(1)
    side = lax.axis_index("yh").astype(jnp.int32).reshape(1)
    swap = [(0, 1), (1, 0)]

    part = features.shape[0] // n_repl
    quarters = call(quarter_kernel, jax.ShapeDtypeStruct((plane, part, EDGE), BF), [SMEM, VMEM])(
        repl, features
    )
    quarters = lax.all_to_all(quarters, PLANE, 0, 0, tiled=True)

    send = call(
        prepare_kernel,
        jax.ShapeDtypeStruct((n_repl, 192, EDGE), BF),
        [SMEM] + [pl.BlockSpec(memory_space=pl.ANY)] * 6,
        [
            pltpu.VMEM((tiles, EDGE, EDGE), jnp.int32),
            pltpu.VMEM((64, EDGE), BF),
            pltpu.VMEM((64, EDGE), BF),
            pltpu.VMEM((CLASSES, 64), BF),
            pltpu.VMEM((CLASSES, 64), BF),
            pltpu.VMEM((1, 64), BF),
            pltpu.VMEM((WIDE, EDGE), F32),
            pltpu.SemaphoreType.DMA((8,)),
            pltpu.SemaphoreType.DMA((5,)),
        ],
        60,
    )(
        tile_blocks,
        tile_counts,
        self_one.T,
        neighbor_one.T,
        neighbor_two.T,
        self_two.T,
        bias_one[None, :],
    )
    quarters, send = lax.optimization_barrier((quarters, send))
    near = lax.all_gather(quarters.reshape(plane * part, EDGE), COLUMN, axis=0, tiled=True)
    got = lax.all_to_all(send, "yl", 0, 0, tiled=True)
    cat = call(lay_kernel, jax.ShapeDtypeStruct((EDGE, tiles * EDGE), BF), [SMEM, VMEM])(
        tile_blocks, tile_counts
    )

    cot = jnp.pad(cotangent, ((0, WIDE - CLASSES), (0, 0)))
    mine, other, up, inv = call(
        spread_kernel,
        (
            jax.ShapeDtypeStruct((plane * halves_n, WIDE, EDGE), F32),
            jax.ShapeDtypeStruct((plane * halves_n, WIDE, EDGE), BF),
            jax.ShapeDtypeStruct((WIDE, EDGE), BF),
            jax.ShapeDtypeStruct((8, EDGE), F32),
        ),
        [SMEM, SMEM] + [VMEM] * 4,
        [pltpu.VMEM((plane * halves_n, WIDE, EDGE), F32)],
    )(tile_blocks, core, cat, got, cot, train_mask[None, :])
    back = call(
        pair_sum_kernel,
        jax.ShapeDtypeStruct((plane * halves_n, WIDE, EDGE), BF),
        [VMEM] * 2,
    )(mine, lax.ppermute(other, "core", swap))
    back = lax.all_to_all(back.reshape(plane, halves_n * WIDE, EDGE), PLANE, 0, 0, tiled=True)
    half = jax.ShapeDtypeStruct((WIDE, EDGE), F32)
    keep, give = call(plane_sum_kernel, (half, half), [SMEM, VMEM])(side, back)
    near, give = lax.optimization_barrier((near, give))
    came = lax.ppermute(give, "yh", swap)
    far = lax.ppermute(near, "core", swap)

    shape = (column, plane, part, EDGE)
    total = call(
        gather_one_kernel,
        jax.ShapeDtypeStruct((EDGE, EDGE), F32),
        [SMEM, SMEM] + [VMEM] * 3,
        [pltpu.VMEM((EDGE, tiles * EDGE), BF)],
    )(tile_blocks, core, near.reshape(shape), far.reshape(shape), cat)
    parts = call(
        mix_kernel, jax.ShapeDtypeStruct((n_repl, EDGE + WIDE, EDGE), BF), [VMEM] * 3
    )(total, keep, came)
    parts = lax.all_to_all(parts, "yl", 0, 0, tiled=True)

    send, base = call(
        layer_kernel,
        (
            jax.ShapeDtypeStruct((sheet, WIDE + 2 * chunk, EDGE), BF),
            jax.ShapeDtypeStruct((WIDE, EDGE), F32),
        ),
        [SMEM] + [VMEM] * 6,
        [pltpu.VMEM((GRADS, EDGE), F32), pltpu.VMEM((8, EDGE), F32)],
    )(repl, parts, got, up, inv, features, bias_two[None, :])
    relay = lax.all_to_all(send, SHEET, 0, 0, tiled=True)
    relay = call(
        relay_kernel,
        jax.ShapeDtypeStruct((sizes["x"], sheet * WIDE + 2 * chunk, EDGE), BF),
        [VMEM],
    )(relay)
    near_two = lax.all_to_all(relay, "x", 0, 0, tiled=True)
    far_two = lax.ppermute(near_two, "core", swap)
    grads = call(
        chunk_sum_kernel, jax.ShapeDtypeStruct((2 * sheet, chunk, EDGE), F32), [VMEM]
    )(near_two[:, sheet * WIDE :])
    grads = lax.all_to_all(grads, SHEET + ("core",), 0, 0, tiled=True)
    second = call(
        functools.partial(gather_two_kernel, sheet),
        jax.ShapeDtypeStruct((WIDE, EDGE), F32),
        [SMEM] * 2 + [VMEM] * 3,
        [pltpu.VMEM((WIDE, tiles * EDGE), BF)],
    )(tile_blocks, core, near_two, far_two, cat)
    others = [
        lax.ppermute(second, "yl", [((i + k) % n_repl, i) for i in range(n_repl)])
        for k in range(1, n_repl)
    ]
    others = others + [second] * (3 - len(others))
    scores = call(
        scores_kernel,
        jax.ShapeDtypeStruct((CLASSES, EDGE), F32),
        [SMEM] + [VMEM] * 6,
        [pltpu.VMEM((n_repl, WIDE, EDGE), F32)],
    )(repl, second, *others, base, inv)
    one = jax.ShapeDtypeStruct((64, EDGE), F32)
    two = jax.ShapeDtypeStruct((CLASSES, 64), F32)
    self_one, neighbor_one, bias_one, self_two, neighbor_two, bias_two = call(
        unpack_kernel,
        (
            one,
            one,
            jax.ShapeDtypeStruct((1, 64), F32),
            two,
            two,
            jax.ShapeDtypeStruct((1, CLASSES), F32),
        ),
        [VMEM],
        [pltpu.VMEM((GRADS, EDGE), F32)],
    )(grads)
    return (
        scores,
        self_one.T,
        neighbor_one.T,
        bias_one[0],
        self_two.T,
        neighbor_two.T,
        bias_two[0],
    )


def solution(mesh):
    sizes = {"x": 4, "z": 8, "yh": 2, "core": 2, "yl": 4}
    fine = Mesh(mesh.devices.reshape(tuple(sizes.values())), tuple(sizes))
    return sharded(fine, sizes)


def sharded(fine, sizes):
    both = ROWS + ("yl",)
    return jax.shard_map(
        functools.partial(per_device, sizes),
        mesh=fine,
        in_specs=(
            P(None, ROWS),
            P(both),
            P(both, None, None),
            P(ROWS),
            P(None, ROWS),
            P(None, "yl"),
            P(None, "yl"),
            P("yl"),
            P("yl", None),
            P("yl", None),
            P(),
        ),
        out_specs=(
            P(None, ROWS),
            P(None, "yl"),
            P(None, "yl"),
            P("yl"),
            P("yl", None),
            P("yl", None),
            P(),
        ),
        check_vma=False,
    )
```

```python
import functools

import jax
import jax.numpy as jnp
from jax import lax
from jax.experimental import pallas as pl
from jax.experimental.pallas import tpu as pltpu
from jax.sharding import Mesh, PartitionSpec as P

BF = jnp.bfloat16
F32 = jnp.float32
CLASSES = 47
WIDE = 48
EDGE = 128
ROWS = ("x", "z", "yh", "core")
PLANE = ("x", "z")
COLUMN = ("yh", "yl")
SHEET = ("z", "yh")
GRADS = 256
VMEM = pl.BlockSpec(memory_space=pltpu.VMEM)
SMEM = pl.BlockSpec(memory_space=pltpu.SMEM)
NT = (((1,), (1,)), ((), ()))
TN = (((0,), (0,)), ((), ()))


def dot(a, b, dims=(((1,), (0,)), ((), ()))):
    return lax.dot_general(a, b, dims, preferred_element_type=F32)


def call(body, outs, in_specs, scratch=(), room=40):
    return pl.pallas_call(
        body,
        out_shape=outs,
        in_specs=in_specs,
        out_specs=jax.tree.map(lambda _: VMEM, outs),
        scratch_shapes=list(scratch),
        compiler_params=pltpu.CompilerParams(vmem_limit_bytes=room * 1024 * 1024),
    )


def halves(value):
    high = value.astype(BF).astype(F32)
    return jnp.concatenate([high, value - high], axis=0).astype(BF)


def quarter_kernel(repl, features, send):
    rows = send.shape[1]
    part = features[pl.ds(pl.multiple_of(repl[0] * rows, 16), rows)]
    for j in range(send.shape[0]):
        send[j] = part


def lay_kernel(blocks, counts, cat):
    for t in range(counts.shape[0]):
        tile = jnp.where(blocks[t] >= 0, counts[t], 0).astype(F32)
        cat[:, t * EDGE : (t + 1) * EDGE] = tile.astype(BF)


def prepare_kernel(blocks, counts, one, two, three, four, five, send, *scratch):
    held, self_one, neighbor_one, neighbor_two, self_two, bias, second, done, ready = scratch
    steps = done.shape[0]
    per = held.shape[0] // steps
    copies = [
        pltpu.make_async_copy(
            counts.at[pl.ds(i * per, per)], held.at[pl.ds(i * per, per)], done.at[i]
        )
        for i in range(steps)
    ]
    pairs = zip((one, two, three, four, five), scratch[1:6])
    weights = [pltpu.make_async_copy(a, b, ready.at[i]) for i, (a, b) in enumerate(pairs)]
    for copy in copies + weights:
        copy.start()
    running = jnp.zeros((EDGE, EDGE), jnp.int32)
    for i, copy in enumerate(copies):
        copy.wait()
        for t in range(i * per, (i + 1) * per):
            running = running + jnp.where(blocks[t] >= 0, held[t], 0)
    for copy in weights:
        copy.wait()
    whole = dot(jnp.ones((8, EDGE), BF), running.astype(F32).astype(BF), NT)[0:1]
    high = jnp.floor(whole * (1.0 / 256.0))
    low = whole - high * 256.0
    row = lax.broadcasted_iota(jnp.int32, (16, EDGE), 0)
    both = jnp.where(row == 0, high, jnp.where(row == 1, low, 0.0)).astype(BF)
    second[...] = jnp.zeros_like(second)
    second[0:CLASSES, 0:64] = neighbor_two[...].astype(F32)
    second[CLASSES:WIDE, 0:64] = bias[...].astype(F32)
    second[0:CLASSES, 64:128] = self_two[...].astype(F32)
    layer_two = second[...].astype(BF)
    for r in range(send.shape[0]):
        send[r, 0:64] = self_one[...]
        send[r, 64:128] = neighbor_one[...]
        send[r, 128:176] = layer_two
        send[r, 176:192] = both


def spread_kernel(blocks, core, cat, got, cot, mask, mine, other, up_out, inv_out, far):
    degree = jnp.zeros((1, EDGE), F32)
    for r in range(got.shape[0]):
        both = got[r, 176:192].astype(F32)
        degree = degree + both[0:1] * 256.0 + both[1:2]
    inverse = 1.0 / (degree + 1.0)
    inv_out[...] = jnp.broadcast_to(inverse, inv_out.shape)
    upstream = cot[...].astype(F32) * mask[...].astype(F32)
    up_out[...] = upstream.astype(BF)
    scaled = (upstream * inverse).astype(BF)
    mine[...] = jnp.zeros_like(mine)
    far[...] = jnp.zeros_like(far)
    me = core[0]
    for t in range(cat.shape[1] // EDGE):
        block = jnp.maximum(blocks[t], 0)
        product = dot(scaled, cat[:, t * EDGE : (t + 1) * EDGE])
        own = (block & 1) == me
        at = block >> 1
        mine[at] += jnp.where(own, product, 0.0)
        far[at] += jnp.where(own, 0.0, product)
    other[...] = far[...].astype(BF)


def pair_sum_kernel(mine, other, total):
    total[...] = (mine[...] + other[...].astype(F32)).astype(BF)


def plane_sum_kernel(side, got, keep, give):
    total = got[0].astype(F32)
    for j in range(1, got.shape[0]):
        total = total + got[j].astype(F32)
    first = side[0] == 0
    keep[...] = jnp.where(first, total[0:WIDE], total[WIDE:])
    give[...] = jnp.where(first, total[WIDE:], total[0:WIDE])


def gather_one_kernel(blocks, core, own, far, cat, total, picked):
    me = core[0]
    part = own.shape[2]
    n_repl = EDGE // part
    for t in range(cat.shape[1] // EDGE):
        block = jnp.maximum(blocks[t], 0)
        half = (block >> 1) & 1
        at = block >> 2
        near = (block & 1) == me
        for q in range(n_repl):
            a = own[half * n_repl + q, at]
            b = far[half * n_repl + q, at]
            picked[q * part : (q + 1) * part, t * EDGE : (t + 1) * EDGE] = jnp.where(near, a, b)
    total[...] = dot(picked[...], cat[...], NT)


def mix_kernel(total, keep, came, send):
    part = halves(total[...])
    terms = (keep[...] + came[...]).astype(BF)
    for r in range(send.shape[0]):
        send[r, 0 : 2 * EDGE] = part
        send[r, 2 * EDGE :] = terms


def layer_kernel(repl, parts, got, up, inv, features, bias_two, send, base, packed, pad):
    chunk = GRADS // send.shape[0]
    n_repl = got.shape[0]
    both = parts[0].astype(F32)
    for r in range(1, n_repl):
        both = both + parts[r].astype(F32)
    mean = ((both[0:EDGE] + both[EDGE : 2 * EDGE]) * inv[0:1]).astype(BF)
    feat = features[...]
    last = lax.broadcasted_iota(jnp.int32, (WIDE, EDGE), 0) == CLASSES
    unit = jnp.where(last, 1.0, 0.0).astype(BF)
    none = jnp.zeros((64, EDGE), BF)

    def before(r):
        bias = dot(got[r, 128:176], unit, TN)[0:64]
        return (dot(got[r, 0:64], feat) + dot(got[r, 64:128], mean)) + bias

    projected = jnp.zeros((WIDE, EDGE), F32)
    skipped = jnp.zeros((WIDE, EDGE), F32)
    for r in range(n_repl):
        pre = before(r)
        hidden = (pre * jax.nn.sigmoid(pre)).astype(BF)
        projected = projected + dot(got[r, 128:176], jnp.concatenate([hidden, none], axis=0))
        skipped = skipped + dot(got[r, 128:176], jnp.concatenate([none, hidden], axis=0))
    projected = projected.astype(BF)
    pad[...] = jnp.zeros_like(pad)
    pad[0:1, 0:CLASSES] = bias_two[...].astype(F32)
    base[...] = skipped + dot(pad[...].astype(BF), jnp.ones((8, EDGE), BF), TN)[0:WIDE]

    pulled = both[2 * EDGE :].astype(BF)
    upstream = up[...]
    mine = repl[0]
    pre = before(mine)
    sigmoid = jax.nn.sigmoid(pre)
    hidden = (pre * sigmoid).astype(BF)
    second = got[mine, 128:176]
    hidden_grad = dot(second, upstream, TN)[64:128] + dot(second, pulled, TN)[0:64]
    pre_grad = (hidden_grad * sigmoid * (1.0 + pre * (1.0 - sigmoid))).astype(BF)
    packed[0:64] = dot(pre_grad, feat, NT)
    packed[64:128] = dot(pre_grad, mean, NT)
    ones = jnp.ones((8, EDGE), BF)
    twice = jnp.concatenate([hidden, hidden], axis=0)
    left = lax.broadcasted_iota(jnp.int32, (WIDE, EDGE), 1) < 64
    grads_two = jnp.where(left, dot(pulled, twice, NT), dot(upstream, twice, NT))
    bias_one = dot(ones, jnp.concatenate([pre_grad, none], axis=0), NT)[0:1]
    packed[128:176] = jnp.where(last, bias_one, grads_two)
    packed[176:184] = dot(ones, jnp.concatenate([upstream, jnp.zeros((EDGE - WIDE, EDGE), BF)], axis=0), NT)
    packed[184:GRADS] = jnp.zeros((GRADS - 184, EDGE), F32)
    for j in range(send.shape[0]):
        send[j, 0:WIDE] = projected
        send[j, WIDE:] = halves(packed[j * chunk : (j + 1) * chunk])


def relay_kernel(got, send):
    sheet = got.shape[0]
    chunk = GRADS // sheet
    total = got[0, WIDE:].astype(F32)
    for j in range(1, sheet):
        total = total + got[j, WIDE:].astype(F32)
    both = halves(total[0:chunk] + total[chunk:])
    for d in range(send.shape[0]):
        for j in range(sheet):
            send[d, j * WIDE : (j + 1) * WIDE] = got[j, 0:WIDE]
        send[d, sheet * WIDE :] = both


def gather_two_kernel(sheet, blocks, core, own, far, cat, send, picked):
    me = core[0]
    for t in range(cat.shape[1] // EDGE):
        block = jnp.maximum(blocks[t], 0)
        place = block >> 1
        line = place // sheet
        rows = pl.ds(pl.multiple_of((place - line * sheet) * WIDE, 16), WIDE)
        near = (block & 1) == me
        a = own[line, rows]
        b = far[line, rows]
        picked[:, t * EDGE : (t + 1) * EDGE] = jnp.where(near, a, b)
    send[...] = dot(picked[...], cat[...], NT)


def chunk_sum_kernel(got, grads):
    chunk = grads.shape[1]
    both = got[0].astype(F32)
    for i in range(1, got.shape[0]):
        both = both + got[i].astype(F32)
    total = both[0:chunk] + both[chunk:]
    for j in range(grads.shape[0]):
        grads[j] = total


def scores_kernel(repl, own, first, second, third, base, inv, scores, parts):
    n_repl = parts.shape[0]
    for k, ref in enumerate((own, first, second, third)[:n_repl]):
        at = repl[0] + k
        parts[jnp.where(at >= n_repl, at - n_repl, at)] = ref[...]
    total = parts[0]
    for r in range(1, n_repl):
        total = total + parts[r]
    scores[...] = (base[...] + total * inv[0:1])[0:CLASSES]


def unpack_kernel(
    got, self_one, neighbor_one, bias_one, self_two, neighbor_two, bias_two, grads
):
    chunk = got.shape[1]
    for j in range(got.shape[0] // 2):
        grads[j * chunk : (j + 1) * chunk] = got[2 * j] + got[2 * j + 1]
    self_one[...] = grads[0:64]
    neighbor_one[...] = grads[64:128]
    neighbor_two[...] = grads[128 : 128 + CLASSES, 0:64]
    self_two[...] = grads[128 : 128 + CLASSES, 64:128]
    bias_one[...] = grads[175:176, 0:64]
    bias_two[...] = grads[176:177, 0:CLASSES]


def per_device(
    sizes,
    features,
    tile_blocks,
    tile_counts,
    train_mask,
    cotangent,
    self_one,
    neighbor_one,
    bias_one,
    self_two,
    neighbor_two,
    bias_two,
):
    n_repl = sizes["yl"]
    plane = sizes["x"] * sizes["z"]
    halves_n = sizes["yh"]
    column = halves_n * n_repl
    tiles = tile_counts.shape[0]
    sheet = sizes["z"] * halves_n
    chunk = GRADS // sheet
    core = lax.axis_index("core").astype(jnp.int32).reshape(1)
    repl = lax.axis_index("yl").astype(jnp.int32).reshape(1)
    side = lax.axis_index("yh").astype(jnp.int32).reshape(1)
    swap = [(0, 1), (1, 0)]

    part = features.shape[0] // n_repl
    quarters = call(quarter_kernel, jax.ShapeDtypeStruct((plane, part, EDGE), BF), [SMEM, VMEM])(
        repl, features
    )
    quarters = lax.all_to_all(quarters, PLANE, 0, 0, tiled=True)

    send = call(
        prepare_kernel,
        jax.ShapeDtypeStruct((n_repl, 192, EDGE), BF),
        [SMEM] + [pl.BlockSpec(memory_space=pl.ANY)] * 6,
        [
            pltpu.VMEM((tiles, EDGE, EDGE), jnp.int32),
            pltpu.VMEM((64, EDGE), BF),
            pltpu.VMEM((64, EDGE), BF),
            pltpu.VMEM((CLASSES, 64), BF),
            pltpu.VMEM((CLASSES, 64), BF),
            pltpu.VMEM((1, 64), BF),
            pltpu.VMEM((WIDE, EDGE), F32),
            pltpu.SemaphoreType.DMA((8,)),
            pltpu.SemaphoreType.DMA((5,)),
        ],
        60,
    )(
        tile_blocks,
        tile_counts,
        self_one.T,
        neighbor_one.T,
        neighbor_two.T,
        self_two.T,
        bias_one[None, :],
    )
    quarters, send = lax.optimization_barrier((quarters, send))
    near = lax.all_gather(quarters.reshape(plane * part, EDGE), COLUMN, axis=0, tiled=True)
    got = lax.all_to_all(send, "yl", 0, 0, tiled=True)
    cat = call(lay_kernel, jax.ShapeDtypeStruct((EDGE, tiles * EDGE), BF), [SMEM, VMEM])(
        tile_blocks, tile_counts
    )

    cot = jnp.pad(cotangent, ((0, WIDE - CLASSES), (0, 0)))
    mine, other, up, inv = call(
        spread_kernel,
        (
            jax.ShapeDtypeStruct((plane * halves_n, WIDE, EDGE), F32),
            jax.ShapeDtypeStruct((plane * halves_n, WIDE, EDGE), BF),
            jax.ShapeDtypeStruct((WIDE, EDGE), BF),
            jax.ShapeDtypeStruct((8, EDGE), F32),
        ),
        [SMEM, SMEM] + [VMEM] * 4,
        [pltpu.VMEM((plane * halves_n, WIDE, EDGE), F32)],
    )(tile_blocks, core, cat, got, cot, train_mask[None, :])
    back = call(
        pair_sum_kernel,
        jax.ShapeDtypeStruct((plane * halves_n, WIDE, EDGE), BF),
        [VMEM] * 2,
    )(mine, lax.ppermute(other, "core", swap))
    back = lax.all_to_all(back.reshape(plane, halves_n * WIDE, EDGE), PLANE, 0, 0, tiled=True)
    half = jax.ShapeDtypeStruct((WIDE, EDGE), F32)
    keep, give = call(plane_sum_kernel, (half, half), [SMEM, VMEM])(side, back)
    near, give = lax.optimization_barrier((near, give))
    came = lax.ppermute(give, "yh", swap)
    far = lax.ppermute(near, "core", swap)

    shape = (column, plane, part, EDGE)
    total = call(
        gather_one_kernel,
        jax.ShapeDtypeStruct((EDGE, EDGE), F32),
        [SMEM, SMEM] + [VMEM] * 3,
        [pltpu.VMEM((EDGE, tiles * EDGE), BF)],
    )(tile_blocks, core, near.reshape(shape), far.reshape(shape), cat)
    parts = call(
        mix_kernel, jax.ShapeDtypeStruct((n_repl, 2 * EDGE + WIDE, EDGE), BF), [VMEM] * 3
    )(total, keep, came)
    parts = lax.all_to_all(parts, "yl", 0, 0, tiled=True)

    send, base = call(
        layer_kernel,
        (
            jax.ShapeDtypeStruct((sheet, WIDE + 2 * chunk, EDGE), BF),
            jax.ShapeDtypeStruct((WIDE, EDGE), F32),
        ),
        [SMEM] + [VMEM] * 6,
        [pltpu.VMEM((GRADS, EDGE), F32), pltpu.VMEM((8, EDGE), F32)],
    )(repl, parts, got, up, inv, features, bias_two[None, :])
    relay = lax.all_to_all(send, SHEET, 0, 0, tiled=True)
    relay = call(
        relay_kernel,
        jax.ShapeDtypeStruct((sizes["x"], sheet * WIDE + 2 * chunk, EDGE), BF),
        [VMEM],
    )(relay)
    near_two = lax.all_to_all(relay, "x", 0, 0, tiled=True)
    far_two = lax.ppermute(near_two, "core", swap)
    grads = call(
        chunk_sum_kernel, jax.ShapeDtypeStruct((2 * sheet, chunk, EDGE), F32), [VMEM]
    )(near_two[:, sheet * WIDE :])
    grads = lax.all_to_all(grads, SHEET + ("core",), 0, 0, tiled=True)
    second = call(
        functools.partial(gather_two_kernel, sheet),
        jax.ShapeDtypeStruct((WIDE, EDGE), F32),
        [SMEM] * 2 + [VMEM] * 3,
        [pltpu.VMEM((WIDE, tiles * EDGE), BF)],
    )(tile_blocks, core, near_two, far_two, cat)
    others = [
        lax.ppermute(second, "yl", [((i + k) % n_repl, i) for i in range(n_repl)])
        for k in range(1, n_repl)
    ]
    others = others + [second] * (3 - len(others))
    scores = call(
        scores_kernel,
        jax.ShapeDtypeStruct((CLASSES, EDGE), F32),
        [SMEM] + [VMEM] * 6,
        [pltpu.VMEM((n_repl, WIDE, EDGE), F32)],
    )(repl, second, *others, base, inv)
    one = jax.ShapeDtypeStruct((64, EDGE), F32)
    two = jax.ShapeDtypeStruct((CLASSES, 64), F32)
    self_one, neighbor_one, bias_one, self_two, neighbor_two, bias_two = call(
        unpack_kernel,
        (
            one,
            one,
            jax.ShapeDtypeStruct((1, 64), F32),
            two,
            two,
            jax.ShapeDtypeStruct((1, CLASSES), F32),
        ),
        [VMEM],
        [pltpu.VMEM((GRADS, EDGE), F32)],
    )(grads)
    return (
        scores,
        self_one.T,
        neighbor_one.T,
        bias_one[0],
        self_two.T,
        neighbor_two.T,
        bias_two[0],
    )


def solution(mesh):
    sizes = {"x": 4, "z": 8, "yh": 2, "core": 2, "yl": 4}
    fine = Mesh(mesh.devices.reshape(tuple(sizes.values())), tuple(sizes))
    return sharded(fine, sizes)


def sharded(fine, sizes):
    both = ROWS + ("yl",)
    return jax.shard_map(
        functools.partial(per_device, sizes),
        mesh=fine,
        in_specs=(
            P(None, ROWS),
            P(both),
            P(both, None, None),
            P(ROWS),
            P(None, ROWS),
            P(None, "yl"),
            P(None, "yl"),
            P("yl"),
            P("yl", None),
            P("yl", None),
            P(),
        ),
        out_specs=(
            P(None, ROWS),
            P(None, "yl"),
            P(None, "yl"),
            P("yl"),
            P("yl", None),
            P("yl", None),
            P(),
        ),
        check_vma=False,
    )
```

```python
import functools

import jax
import jax.numpy as jnp
from jax import lax
from jax.experimental import pallas as pl
from jax.experimental.pallas import tpu as pltpu
from jax.sharding import Mesh, PartitionSpec as P

BF = jnp.bfloat16
F32 = jnp.float32
CLASSES = 47
WIDE = 48
EDGE = 128
ROWS = ("x", "z", "yh", "core")
PLANE = ("x", "z")
COLUMN = ("yh", "yl")
SHEET = ("z", "yh")
GRADS = 256
VMEM = pl.BlockSpec(memory_space=pltpu.VMEM)
SMEM = pl.BlockSpec(memory_space=pltpu.SMEM)
NT = (((1,), (1,)), ((), ()))
TN = (((0,), (0,)), ((), ()))


def dot(a, b, dims=(((1,), (0,)), ((), ()))):
    return lax.dot_general(a, b, dims, preferred_element_type=F32)


def call(body, outs, in_specs, scratch=(), room=40):
    return pl.pallas_call(
        body,
        out_shape=outs,
        in_specs=in_specs,
        out_specs=jax.tree.map(lambda _: VMEM, outs),
        scratch_shapes=list(scratch),
        compiler_params=pltpu.CompilerParams(vmem_limit_bytes=room * 1024 * 1024),
    )


def halves(value):
    high = value.astype(BF).astype(F32)
    return jnp.concatenate([high, value - high], axis=0).astype(BF)


def quarter_kernel(repl, features, send):
    rows = send.shape[1]
    part = features[pl.ds(pl.multiple_of(repl[0] * rows, 16), rows)]
    for j in range(send.shape[0]):
        send[j] = part


def lay_kernel(blocks, counts, cat):
    for t in range(counts.shape[0]):
        tile = jnp.where(blocks[t] >= 0, counts[t], 0).astype(F32)
        cat[:, t * EDGE : (t + 1) * EDGE] = tile.astype(BF)


def prepare_kernel(blocks, counts, one, two, three, four, five, send, *scratch):
    held, self_one, neighbor_one, neighbor_two, self_two, bias, second, done, ready = scratch
    steps = done.shape[0]
    per = held.shape[0] // steps
    copies = [
        pltpu.make_async_copy(
            counts.at[pl.ds(i * per, per)], held.at[pl.ds(i * per, per)], done.at[i]
        )
        for i in range(steps)
    ]
    pairs = zip((one, two, three, four, five), scratch[1:6])
    weights = [pltpu.make_async_copy(a, b, ready.at[i]) for i, (a, b) in enumerate(pairs)]
    for copy in copies + weights:
        copy.start()
    running = jnp.zeros((EDGE, EDGE), jnp.int32)
    for i, copy in enumerate(copies):
        copy.wait()
        for t in range(i * per, (i + 1) * per):
            running = running + jnp.where(blocks[t] >= 0, held[t], 0)
    for copy in weights:
        copy.wait()
    whole = dot(jnp.ones((8, EDGE), BF), running.astype(F32).astype(BF), NT)[0:1]
    high = jnp.floor(whole * (1.0 / 256.0))
    low = whole - high * 256.0
    row = lax.broadcasted_iota(jnp.int32, (16, EDGE), 0)
    both = jnp.where(row == 0, high, jnp.where(row == 1, low, 0.0)).astype(BF)
    second[...] = jnp.zeros_like(second)
    second[0:CLASSES, 0:64] = neighbor_two[...].astype(F32)
    second[CLASSES:WIDE, 0:64] = bias[...].astype(F32)
    second[0:CLASSES, 64:128] = self_two[...].astype(F32)
    layer_two = second[...].astype(BF)
    for r in range(send.shape[0]):
        send[r, 0:64] = self_one[...]
        send[r, 64:128] = neighbor_one[...]
        send[r, 128:176] = layer_two
        send[r, 176:192] = both


def spread_kernel(blocks, core, cat, got, cot, mask, mine, other, up_out, inv_out, far):
    degree = jnp.zeros((1, EDGE), F32)
    for r in range(got.shape[0]):
        both = got[r, 176:192].astype(F32)
        degree = degree + both[0:1] * 256.0 + both[1:2]
    inverse = 1.0 / (degree + 1.0)
    inv_out[...] = jnp.broadcast_to(inverse, inv_out.shape)
    upstream = cot[...].astype(F32) * mask[...].astype(F32)
    up_out[...] = upstream.astype(BF)
    scaled = (upstream * inverse).astype(BF)
    mine[...] = jnp.zeros_like(mine)
    far[...] = jnp.zeros_like(far)
    me = core[0]
    for t in range(cat.shape[1] // EDGE):
        block = jnp.maximum(blocks[t], 0)
        product = dot(scaled, cat[:, t * EDGE : (t + 1) * EDGE])
        own = (block & 1) == me
        at = block >> 1
        mine[at] += jnp.where(own, product, 0.0)
        far[at] += jnp.where(own, 0.0, product)
    other[...] = far[...].astype(BF)


def pair_sum_kernel(mine, other, total):
    total[...] = (mine[...] + other[...].astype(F32)).astype(BF)


def plane_sum_kernel(side, got, keep, give):
    total = got[0].astype(F32)
    for j in range(1, got.shape[0]):
        total = total + got[j].astype(F32)
    first = side[0] == 0
    keep[...] = jnp.where(first, total[0:WIDE], total[WIDE:])
    give[...] = jnp.where(first, total[WIDE:], total[0:WIDE])


def gather_one_kernel(blocks, core, own, far, cat, total, picked):
    me = core[0]
    part = own.shape[2]
    n_repl = EDGE // part
    for t in range(cat.shape[1] // EDGE):
        block = jnp.maximum(blocks[t], 0)
        half = (block >> 1) & 1
        at = block >> 2
        near = (block & 1) == me
        for q in range(n_repl):
            a = own[half * n_repl + q, at]
            b = far[half * n_repl + q, at]
            picked[q * part : (q + 1) * part, t * EDGE : (t + 1) * EDGE] = jnp.where(near, a, b)
    total[...] = dot(picked[...], cat[...], NT)


def mix_kernel(total, keep, came, send):
    part = halves(total[...])
    terms = (keep[...] + came[...]).astype(BF)
    for r in range(send.shape[0]):
        send[r, 0 : 2 * EDGE] = part
        send[r, 2 * EDGE :] = terms


def layer_kernel(repl, parts, got, up, inv, features, bias_two, send, base, packed, pad):
    chunk = GRADS // send.shape[0]
    n_repl = got.shape[0]
    both = parts[0].astype(F32)
    for r in range(1, n_repl):
        both = both + parts[r].astype(F32)
    mean = ((both[0:EDGE] + both[EDGE : 2 * EDGE]) * inv[0:1]).astype(BF)
    feat = features[...]
    last = lax.broadcasted_iota(jnp.int32, (WIDE, EDGE), 0) == CLASSES
    unit = jnp.where(last, 1.0, 0.0).astype(BF)
    none = jnp.zeros((64, EDGE), BF)

    def before(r):
        bias = dot(got[r, 128:176], unit, TN)[0:64]
        return (dot(got[r, 0:64], feat) + dot(got[r, 64:128], mean)) + bias

    projected = jnp.zeros((WIDE, EDGE), F32)
    skipped = jnp.zeros((WIDE, EDGE), F32)
    for r in range(n_repl):
        pre = before(r)
        hidden = (pre * jax.nn.sigmoid(pre)).astype(BF)
        projected = projected + dot(got[r, 128:176], jnp.concatenate([hidden, none], axis=0))
        skipped = skipped + dot(got[r, 128:176], jnp.concatenate([none, hidden], axis=0))
    projected = projected.astype(BF)
    pad[...] = jnp.zeros_like(pad)
    pad[0:1, 0:CLASSES] = bias_two[...].astype(F32)
    base[...] = skipped + dot(pad[...].astype(BF), jnp.ones((8, EDGE), BF), TN)[0:WIDE]

    pulled = both[2 * EDGE :].astype(BF)
    upstream = up[...]
    mine = repl[0]
    pre = before(mine)
    sigmoid = jax.nn.sigmoid(pre)
    hidden = (pre * sigmoid).astype(BF)
    second = got[mine, 128:176]
    hidden_grad = dot(second, upstream, TN)[64:128] + dot(second, pulled, TN)[0:64]
    pre_grad = (hidden_grad * sigmoid * (1.0 + pre * (1.0 - sigmoid))).astype(BF)
    packed[0:64] = dot(pre_grad, feat, NT)
    packed[64:128] = dot(pre_grad, mean, NT)
    ones = jnp.ones((8, EDGE), BF)
    twice = jnp.concatenate([hidden, hidden], axis=0)
    left = lax.broadcasted_iota(jnp.int32, (WIDE, EDGE), 1) < 64
    grads_two = jnp.where(left, dot(pulled, twice, NT), dot(upstream, twice, NT))
    bias_one = dot(ones, jnp.concatenate([pre_grad, none], axis=0), NT)[0:1]
    packed[128:176] = jnp.where(last, bias_one, grads_two)
    packed[176:184] = dot(ones, jnp.concatenate([upstream, jnp.zeros((EDGE - WIDE, EDGE), BF)], axis=0), NT)
    packed[184:GRADS] = jnp.zeros((GRADS - 184, EDGE), F32)
    for j in range(send.shape[0]):
        send[j, 0:WIDE] = projected
        send[j, WIDE:] = halves(packed[j * chunk : (j + 1) * chunk])


def relay_kernel(got, send):
    sheet = got.shape[0]
    chunk = GRADS // sheet
    total = got[0, WIDE:].astype(F32)
    for j in range(1, sheet):
        total = total + got[j, WIDE:].astype(F32)
    both = halves(total[0:chunk] + total[chunk:])
    for d in range(send.shape[0]):
        for j in range(sheet):
            send[d, j * WIDE : (j + 1) * WIDE] = got[j, 0:WIDE]
        send[d, sheet * WIDE :] = both


def gather_two_kernel(sheet, blocks, core, own, far, cat, send, picked):
    me = core[0]
    for t in range(cat.shape[1] // EDGE):
        block = jnp.maximum(blocks[t], 0)
        place = block >> 1
        line = place // sheet
        rows = pl.ds(pl.multiple_of((place - line * sheet) * WIDE, 16), WIDE)
        near = (block & 1) == me
        a = own[line, rows]
        b = far[line, rows]
        picked[:, t * EDGE : (t + 1) * EDGE] = jnp.where(near, a, b)
    send[...] = dot(picked[...], cat[...], NT)


def chunk_sum_kernel(got, grads):
    chunk = grads.shape[1]
    both = got[0].astype(F32)
    for i in range(1, got.shape[0]):
        both = both + got[i].astype(F32)
    total = both[0:chunk] + both[chunk:]
    for j in range(grads.shape[0]):
        grads[j] = total


def scores_kernel(repl, own, first, second, third, base, inv, scores, parts):
    n_repl = parts.shape[0]
    for k, ref in enumerate((own, first, second, third)[:n_repl]):
        at = repl[0] + k
        parts[jnp.where(at >= n_repl, at - n_repl, at)] = ref[...]
    total = parts[0]
    for r in range(1, n_repl):
        total = total + parts[r]
    scores[...] = (base[...] + total * inv[0:1])[0:CLASSES]


def unpack_kernel(
    got, self_one, neighbor_one, bias_one, self_two, neighbor_two, bias_two, grads
):
    chunk = got.shape[1]
    for j in range(got.shape[0] // 2):
        grads[j * chunk : (j + 1) * chunk] = got[2 * j] + got[2 * j + 1]
    self_one[...] = grads[0:64]
    neighbor_one[...] = grads[64:128]
    neighbor_two[...] = grads[128 : 128 + CLASSES, 0:64]
    self_two[...] = grads[128 : 128 + CLASSES, 64:128]
    bias_one[...] = grads[175:176, 0:64]
    bias_two[...] = grads[176:177, 0:CLASSES]


def per_device(
    sizes,
    features,
    tile_blocks,
    tile_counts,
    train_mask,
    cotangent,
    self_one,
    neighbor_one,
    bias_one,
    self_two,
    neighbor_two,
    bias_two,
):
    n_repl = sizes["yl"]
    plane = sizes["x"] * sizes["z"]
    halves_n = sizes["yh"]
    column = halves_n * n_repl
    tiles = tile_counts.shape[0]
    sheet = sizes["z"] * halves_n
    chunk = GRADS // sheet
    core = lax.axis_index("core").astype(jnp.int32).reshape(1)
    repl = lax.axis_index("yl").astype(jnp.int32).reshape(1)
    side = lax.axis_index("yh").astype(jnp.int32).reshape(1)
    swap = [(0, 1), (1, 0)]

    part = features.shape[0] // n_repl
    quarters = call(quarter_kernel, jax.ShapeDtypeStruct((plane, part, EDGE), BF), [SMEM, VMEM])(
        repl, features
    )
    quarters = lax.all_to_all(quarters, PLANE, 0, 0, tiled=True)

    send = call(
        prepare_kernel,
        jax.ShapeDtypeStruct((n_repl, 192, EDGE), BF),
        [SMEM] + [pl.BlockSpec(memory_space=pl.ANY)] * 6,
        [
            pltpu.VMEM((tiles, EDGE, EDGE), jnp.int32),
            pltpu.VMEM((64, EDGE), BF),
            pltpu.VMEM((64, EDGE), BF),
            pltpu.VMEM((CLASSES, 64), BF),
            pltpu.VMEM((CLASSES, 64), BF),
            pltpu.VMEM((1, 64), BF),
            pltpu.VMEM((WIDE, EDGE), F32),
            pltpu.SemaphoreType.DMA((8,)),
            pltpu.SemaphoreType.DMA((5,)),
        ],
        60,
    )(
        tile_blocks,
        tile_counts,
        self_one.T,
        neighbor_one.T,
        neighbor_two.T,
        self_two.T,
        bias_one[None, :],
    )
    quarters, send = lax.optimization_barrier((quarters, send))
    near = lax.all_gather(quarters.reshape(plane * part, EDGE), COLUMN, axis=0, tiled=True)
    got = lax.all_to_all(send, "yl", 0, 0, tiled=True)
    cat = call(lay_kernel, jax.ShapeDtypeStruct((EDGE, tiles * EDGE), BF), [SMEM, VMEM])(
        tile_blocks, tile_counts
    )

    cot = jnp.pad(cotangent, ((0, WIDE - CLASSES), (0, 0)))
    mine, other, up, inv = call(
        spread_kernel,
        (
            jax.ShapeDtypeStruct((plane * halves_n, WIDE, EDGE), F32),
            jax.ShapeDtypeStruct((plane * halves_n, WIDE, EDGE), BF),
            jax.ShapeDtypeStruct((WIDE, EDGE), BF),
            jax.ShapeDtypeStruct((8, EDGE), F32),
        ),
        [SMEM, SMEM] + [VMEM] * 4,
        [pltpu.VMEM((plane * halves_n, WIDE, EDGE), F32)],
    )(tile_blocks, core, cat, got, cot, train_mask[None, :])
    back = call(
        pair_sum_kernel,
        jax.ShapeDtypeStruct((plane * halves_n, WIDE, EDGE), BF),
        [VMEM] * 2,
    )(mine, lax.ppermute(other, "core", swap))
    back = lax.all_to_all(back.reshape(plane, halves_n * WIDE, EDGE), PLANE, 0, 0, tiled=True)
    half = jax.ShapeDtypeStruct((WIDE, EDGE), F32)
    keep, give = call(plane_sum_kernel, (half, half), [SMEM, VMEM])(side, back)
    late, give = lax.optimization_barrier((near, give))
    came = lax.ppermute(give, "yh", swap)
    far = lax.ppermute(late, "core", swap)

    shape = (column, plane, part, EDGE)
    total = call(
        gather_one_kernel,
        jax.ShapeDtypeStruct((EDGE, EDGE), F32),
        [SMEM, SMEM] + [VMEM] * 3,
        [pltpu.VMEM((EDGE, tiles * EDGE), BF)],
    )(tile_blocks, core, near.reshape(shape), far.reshape(shape), cat)
    parts = call(
        mix_kernel, jax.ShapeDtypeStruct((n_repl, 2 * EDGE + WIDE, EDGE), BF), [VMEM] * 3
    )(total, keep, came)
    parts = lax.all_to_all(parts, "yl", 0, 0, tiled=True)

    send, base = call(
        layer_kernel,
        (
            jax.ShapeDtypeStruct((sheet, WIDE + 2 * chunk, EDGE), BF),
            jax.ShapeDtypeStruct((WIDE, EDGE), F32),
        ),
        [SMEM] + [VMEM] * 6,
        [pltpu.VMEM((GRADS, EDGE), F32), pltpu.VMEM((8, EDGE), F32)],
    )(repl, parts, got, up, inv, features, bias_two[None, :])
    relay = lax.all_to_all(send, SHEET, 0, 0, tiled=True)
    relay = call(
        relay_kernel,
        jax.ShapeDtypeStruct((sizes["x"], sheet * WIDE + 2 * chunk, EDGE), BF),
        [VMEM],
    )(relay)
    near_two = lax.all_to_all(relay, "x", 0, 0, tiled=True)
    far_two = lax.ppermute(near_two, "core", swap)
    grads = call(
        chunk_sum_kernel, jax.ShapeDtypeStruct((2 * sheet, chunk, EDGE), F32), [VMEM]
    )(near_two[:, sheet * WIDE :])
    grads = lax.all_to_all(grads, SHEET + ("core",), 0, 0, tiled=True)
    second = call(
        functools.partial(gather_two_kernel, sheet),
        jax.ShapeDtypeStruct((WIDE, EDGE), F32),
        [SMEM] * 2 + [VMEM] * 3,
        [pltpu.VMEM((WIDE, tiles * EDGE), BF)],
    )(tile_blocks, core, near_two, far_two, cat)
    others = [
        lax.ppermute(second, "yl", [((i + k) % n_repl, i) for i in range(n_repl)])
        for k in range(1, n_repl)
    ]
    others = others + [second] * (3 - len(others))
    scores = call(
        scores_kernel,
        jax.ShapeDtypeStruct((CLASSES, EDGE), F32),
        [SMEM] + [VMEM] * 6,
        [pltpu.VMEM((n_repl, WIDE, EDGE), F32)],
    )(repl, second, *others, base, inv)
    one = jax.ShapeDtypeStruct((64, EDGE), F32)
    two = jax.ShapeDtypeStruct((CLASSES, 64), F32)
    self_one, neighbor_one, bias_one, self_two, neighbor_two, bias_two = call(
        unpack_kernel,
        (
            one,
            one,
            jax.ShapeDtypeStruct((1, 64), F32),
            two,
            two,
            jax.ShapeDtypeStruct((1, CLASSES), F32),
        ),
        [VMEM],
        [pltpu.VMEM((GRADS, EDGE), F32)],
    )(grads)
    return (
        scores,
        self_one.T,
        neighbor_one.T,
        bias_one[0],
        self_two.T,
        neighbor_two.T,
        bias_two[0],
    )


def solution(mesh):
    sizes = {"x": 4, "z": 8, "yh": 2, "core": 2, "yl": 4}
    fine = Mesh(mesh.devices.reshape(tuple(sizes.values())), tuple(sizes))
    return sharded(fine, sizes)


def sharded(fine, sizes):
    both = ROWS + ("yl",)
    return jax.shard_map(
        functools.partial(per_device, sizes),
        mesh=fine,
        in_specs=(
            P(None, ROWS),
            P(both),
            P(both, None, None),
            P(ROWS),
            P(None, ROWS),
            P(None, "yl"),
            P(None, "yl"),
            P("yl"),
            P("yl", None),
            P("yl", None),
            P(),
        ),
        out_specs=(
            P(None, ROWS),
            P(None, "yl"),
            P(None, "yl"),
            P("yl"),
            P("yl", None),
            P("yl", None),
            P(),
        ),
        check_vma=False,
    )
```
